256 devices in a mesh: east: 16 (over y, z_hi), north: 16 (over z_lo, x, core).
Axes of the slice: x: 4, y: 4, z: 8 (z_hi: 4, z_lo: 2; z = z_hi * 2 + z_lo), core: 2. Of those that a mesh axis runs over, the one named last changes fastest.
Arguments:
- head_old: float32 [64, 256, 2048], P(None, 'east', 'north'), may hold values from -6 to 6
- source: float32 [64, 256, 2048], P(None, 'east', 'north'), may hold values from -6 to 6
- mode_coeffs: float32 [8, 8, 8], replicated, may hold values from -4 to 4
- records: float32 [32, 1048576], P(None, ('east', 'north')), may hold values from -6 to 6
- cell_index: int32 [1048576], P(('east', 'north')), may hold values from 0 to 131071
- coupling: float32 [3, 32], replicated, may hold values from -3.5 to 3.5
- send_list: int32 [4, 131072], P(None, ('east', 'north')), may hold values from 0 to 4095, as said below
- send_count: int32 [4, 256], P(None, ('east', 'north')), may hold values from 0 to 512, as said below
Outputs:
- heads: float32 [64, 256, 2048], P(None, 'east', 'north')
- moved: float32 [32, 1048576], P(None, ('east', 'north'))
- arrivals: float32 [4, 32, 131072], P(None, None, ('east', 'north'))
The draws below stay inside these ranges and needn't reach their ends.
Inputs may be any that keep to these rules, and one draw needn't show every extreme that they name: `send_list`: within one tile's block the 512 slots of all four directions name distinct particles of that tile. `send_count`: some tile fills all 512 slots of some direction.
All inputs are finite; a program needn't handle non-finite values.
Results may differ from the reference program's by a relative error of at most 0.000076.
Values sent between devices are 32-bit elements; how exact they have to be, the bound alone decides.
No kernel may reach another device: no remote copies, remote signals or barrier semaphores. Data moves between devices by JAX's collectives and lax.ppermute only.
A program may use at most 64 MiB of HBM per device.

```python
import jax
import jax.numpy as jnp
from jax import lax

CX = 16
CY = 128
LAYERS = 64
ITERS = 4
MODES_Z = 8
MODES_X = 8
MODES_Y = 8
RECORD = 32
P_DEV = 4096
CAP = 512
TILES = 256
NX = 256
NY = 2048
N_EAST = 16
N_NORTH = 16


def draw_send_list(key, part):
    tile_keys = jax.random.split(key, TILES)

    def one_tile(tile_key):
        return jax.random.permutation(tile_key, P_DEV)[:4 * CAP].reshape(4, CAP)
    lists = jax.vmap(one_tile)(tile_keys)
    return jnp.transpose(lists, (1, 0, 2)).reshape(4, TILES * CAP).astype(jnp.int32)


def draw_send_count(key, part):
    first_key, second_key, third_key = jax.random.split(jax.random.fold_in(key, 7), 3)
    first = jax.random.randint(first_key, (4, TILES), 0, CAP + 1)
    second = jax.random.randint(second_key, (4, TILES), 0, CAP + 1)
    counts = jnp.maximum(first, second).reshape(-1)
    chosen = jax.random.randint(third_key, (), 0, 4 * TILES)
    counts = counts.at[chosen].set(CAP)
    return counts.reshape(4, TILES).astype(jnp.int32)


def touch_ends(result, rng, smallest, high):
    extent = result.shape
    index_at = [jax.random.randint(jax.random.fold_in(rng, axis), (), 0, extent[axis]) for axis in range(len(extent))]
    result = result.at[tuple(index_at)].set(smallest)
    longest = extent.index(max(extent))
    index_at[longest] = (index_at[longest] + 1) % extent[longest]
    return result.at[tuple(index_at)].set(high)


def shard_levels(own_key, dims, cuts, least, top_value):
    loudness = 1.0
    for dim, parts in cuts:
        draws = jax.random.uniform(jax.random.fold_in(jax.random.fold_in(own_key, 6), dim), (parts,), jnp.float32, least / len(cuts), top_value / len(cuts))
        loudness = loudness * jnp.repeat(jnp.exp(draws), dims[dim] // parts).reshape((-1,) + (1,) * (len(dims) - 1 - dim))
    return loudness


def noise(own_key, dims, scale, limit, cuts=(), held_as=jnp.bfloat16):
    entries = jax.random.normal(own_key, dims, jnp.float32) * scale
    if len(cuts) > 0:
        entries = shard_levels(own_key, dims, cuts, -0.22, 0.18) * entries
    return jnp.clip(entries, min=-limit, max=limit).astype(held_as)


def setup_inputs(seed: int = 0) -> dict:
    splits = jax.random.split(jax.random.key(seed), 9)
    head_old = noise(splits[0], (LAYERS, NX, NY), 1.0, 6.0, ((1, 16), (2, 16)), jnp.float32)
    source = noise(splits[1], (LAYERS, NX, NY), 1.0, 6.0, ((1, 16), (2, 16)), jnp.float32)
    mode_coeffs = noise(splits[2], (MODES_Z, MODES_X, MODES_Y), 1.0, 4.0, (), jnp.float32)
    records = noise(splits[3], (RECORD, P_DEV * TILES), 1.0, 6.0, ((1, 256),), jnp.float32)
    cell_index = touch_ends(jax.random.randint(splits[4], (P_DEV * TILES,), 0, LAYERS * CX * CY), jax.random.fold_in(splits[4], 1), 0, (LAYERS * CX * CY) - 1).astype(jnp.int32)
    coupling = noise(splits[5], (3, RECORD), 3 ** -0.5, 3.5, (), jnp.float32)
    send_list = draw_send_list(jax.random.fold_in(splits[8], 71), 0)
    send_count = draw_send_count(jax.random.fold_in(splits[8], 71), 0)
    return dict(head_old=head_old, source=source, mode_coeffs=mode_coeffs, records=records, cell_index=cell_index, coupling=coupling, send_list=send_list, send_count=send_count)


gardner_rate = 1.0
step_size = 0.25
mean_log = 0.0
spread_log = 1.0
highest = lax.Precision.HIGHEST

def mode_table(coords, count, total):
    orders = jnp.arange(count).astype(jnp.float32)
    return jnp.cos(jnp.pi * orders[:, None] * (coords.astype(jnp.float32)[None, :] + 0.5) / total)

def mode_weights(mode_coeffs):
    order_z = jnp.arange(mode_coeffs.shape[0]).astype(jnp.float32)
    order_x = jnp.arange(mode_coeffs.shape[1]).astype(jnp.float32)
    order_y = jnp.arange(mode_coeffs.shape[2]).astype(jnp.float32)
    spectrum = 1.0 / (1.0 + (order_z[:, None, None] ** 2 + order_x[None, :, None] ** 2 + order_y[None, None, :] ** 2) / 4.0)
    return mode_coeffs * jnp.sqrt(spectrum) * (spread_log / jnp.sqrt(jnp.sum(spectrum)))

def conductivity(weights, table_z, table_x, table_y):
    partial_y = jnp.einsum('cab,by->cay', weights, table_y, precision=highest)
    partial_x = jnp.einsum('cay,ax->cxy', partial_y, table_x, precision=highest)
    return jnp.exp(mean_log + jnp.einsum('cl,cxy->lxy', table_z, partial_x, precision=highest))

def relative(head_field):
    return jnp.exp(gardner_rate * jnp.minimum(head_field, 0.0))

def jacobi_sweep(head_field, cond, storage, head_old, source):
    darcy_k = cond * relative(head_field)
    zero_x = jnp.zeros_like(darcy_k[:, :1, :])
    faces_x = 0.5 * (darcy_k[:, 1:, :] + darcy_k[:, :-1, :])
    face_east = jnp.concatenate([faces_x, zero_x], 1)
    face_west = jnp.concatenate([zero_x, faces_x], 1)
    head_east = jnp.concatenate([head_field[:, 1:, :], zero_x], 1)
    head_west = jnp.concatenate([zero_x, head_field[:, :-1, :]], 1)
    zero_y = jnp.zeros_like(darcy_k[:, :, :1])
    faces_y = 0.5 * (darcy_k[:, :, 1:] + darcy_k[:, :, :-1])
    face_north = jnp.concatenate([faces_y, zero_y], 2)
    face_south = jnp.concatenate([zero_y, faces_y], 2)
    head_north = jnp.concatenate([head_field[:, :, 1:], zero_y], 2)
    head_south = jnp.concatenate([zero_y, head_field[:, :, :-1]], 2)
    zero_z = jnp.zeros_like(darcy_k[:1])
    faces_z = 0.5 * (darcy_k[1:] + darcy_k[:-1])
    face_up = jnp.concatenate([faces_z, zero_z], 0)
    face_down = jnp.concatenate([zero_z, faces_z], 0)
    head_up = jnp.concatenate([head_field[1:], zero_z], 0)
    head_down = jnp.concatenate([zero_z, head_field[:-1]], 0)
    numerator = storage * head_old + face_east * head_east + face_west * head_west + face_north * head_north + face_south * head_south + face_up * head_up + face_down * head_down + face_up - face_down + source
    denominator = storage + face_east + face_west + face_north + face_south + face_up + face_down
    return numerator / denominator

def darcy_velocity(head_field, cond):
    darcy_k = cond * relative(head_field)
    padded = jnp.pad(head_field, 1)
    flow_x = -darcy_k * 0.5 * (padded[1:-1, 2:, 1:-1] - padded[1:-1, :-2, 1:-1])
    flow_y = -darcy_k * 0.5 * (padded[1:-1, 1:-1, 2:] - padded[1:-1, 1:-1, :-2])
    flow_z = -darcy_k * (0.5 * (padded[2:, 1:-1, 1:-1] - padded[:-2, 1:-1, 1:-1]) + 1.0)
    return jnp.stack([flow_x, flow_y, flow_z])

def reference(head_old, source, mode_coeffs, records, cell_index, coupling, send_list, send_count):
    weights = mode_weights(mode_coeffs)
    cond = conductivity(weights, mode_table(jnp.arange(LAYERS), mode_coeffs.shape[0], LAYERS), mode_table(jnp.arange(NX), mode_coeffs.shape[1], NX), mode_table(jnp.arange(NY), mode_coeffs.shape[2], NY))
    storage = 0.5 + 0.5 * relative(head_old)
    head_field = head_old
    for number in range(ITERS):
        head_field = jacobi_sweep(head_field, cond, storage, head_old, source)
    velocity = darcy_velocity(head_field, cond)
    particle = jnp.arange(TILES * P_DEV).astype(jnp.int32)
    tile_of = particle // P_DEV
    layer_of = cell_index // (CX * CY)
    row_x = tile_of // N_NORTH * CX + cell_index // CY % CX
    row_y = tile_of % N_NORTH * CY + cell_index % CY
    sampled = velocity[:, layer_of, row_x, row_y]
    moved = records + step_size * jnp.dot(coupling.T, sampled, precision=highest)
    offsets = (jnp.arange(TILES) * P_DEV).astype(jnp.int32)
    global_lists = send_list.reshape(4, TILES, CAP) + offsets[None, :, None]
    picked = moved[:, global_lists]
    live_slots = (jnp.arange(CAP).astype(jnp.int32)[None, None, :] < send_count[:, :, None]).astype(jnp.float32)
    buffers = jnp.transpose(picked, (1, 0, 2, 3)) * live_slots[:, None]
    tile_grid = buffers.reshape(4, RECORD, N_EAST, N_NORTH, CAP)
    empty_east = jnp.zeros((RECORD, 1, N_NORTH, CAP), jnp.float32)
    empty_north = jnp.zeros((RECORD, N_EAST, 1, CAP), jnp.float32)
    from_low_east = jnp.concatenate([empty_east, tile_grid[0, :, :-1]], 1)
    from_high_east = jnp.concatenate([tile_grid[1, :, 1:], empty_east], 1)
    from_low_north = jnp.concatenate([empty_north, tile_grid[2, :, :, :-1]], 2)
    from_high_north = jnp.concatenate([tile_grid[3, :, :, 1:], empty_north], 2)
    arrivals = jnp.stack([from_low_east, from_high_east, from_low_north, from_high_north]).reshape(4, RECORD, TILES * CAP)
    return (head_field, moved, arrivals)
```

```python
import functools

import jax
import jax.numpy as jnp
from jax import lax
from jax.experimental import pallas as pl
from jax.experimental.pallas import tpu as pltpu
from jax.sharding import PartitionSpec as P

ITERS = 4
LZ, CX, CY = 64, 16, 128
HALF = CY // 2
WIDE = ITERS + 1
EXT = CX + 2 * WIDE
ROWS = HALF + 16
PAD = ROWS + 16
NX, NY = 256, 2048
NSIDE = WIDE - 1
ESEND = WIDE * HALF + NSIDE * HALF + 2 * NSIDE * 8
STEP = 0.25
F32 = jnp.float32
VMEM = pl.BlockSpec(memory_space=pltpu.VMEM)
SMEM = pl.BlockSpec(memory_space=pltpu.SMEM)


def lanes(shape):
    return lax.broadcasted_iota(jnp.int32, shape, len(shape) - 1)


def swap(v):
    return pltpu.roll(v, 64, 1)


def turn_kernel(h_ref, s_ref, ht_ref, st_ref, nlo_ref, nhi_ref):
    low = lanes((8, 128)) < 64

    def turned(ref, x):
        t = ref[pl.ds(x, LZ, stride=CX), :].T
        return jnp.concatenate([t[:HALF], t[HALF:]], axis=1)

    for x in range(CX):
        h, s = turned(h_ref, x), turned(s_ref, x)
        ht_ref[x] = h
        st_ref[x] = s
        nlo_ref[x] = jnp.where(low, swap(h[HALF - 8 :]), s[HALF - 8 :])
        nhi_ref[x] = jnp.where(low, h[:8], swap(s[:8]))


def pack_kernel(ht_ref, st_ref, nlo_ref, nhi_ref, elo_ref, ehi_ref):
    for ref, at, at_s in ((elo_ref, CX - WIDE, CX - NSIDE), (ehi_ref, 0, 0)):
        row = 0
        for source, start, count in (
            (ht_ref, at, WIDE),
            (st_ref, at_s, NSIDE),
            (nlo_ref, at_s, NSIDE),
            (nhi_ref, at_s, NSIDE),
        ):
            height = source.shape[1]
            for i in range(count):
                ref[row : row + height] = source[start + i]
                row += height


def cond_kernel(w_ref, out_ref, base_ref, xrow_ref):
    start_x = lax.axis_index("east") * CX - WIDE
    start_y = lax.axis_index("north") * CY - 8
    lane = lanes((ROWS, 128))
    row = lax.broadcasted_iota(jnp.int32, (ROWS, 128), 0)
    y = start_y + row + (lane // 64) * HALF
    inside_y = (y >= 0) & (y < NY)
    coord = y.astype(F32) + 0.5
    base = jnp.broadcast_to(w_ref[0:1, :], (ROWS, 128))
    for b in range(1, 8):
        base = base + w_ref[b : b + 1, :] * jnp.cos(jnp.pi * float(b) * coord / NY)
    base_ref[...] = base
    lane_x = lanes((32, 128))
    x = start_x + lax.broadcasted_iota(jnp.int32, (32, 128), 0)
    order = (lane_x % 8).astype(F32)
    xrow_ref[...] = jnp.cos(jnp.pi * order * (x.astype(F32) + 0.5) / NX)
    lane_z = lanes((128, 128))
    mode = lax.broadcasted_iota(jnp.int32, (128, 128), 0)
    order = ((mode % 64) // 8).astype(F32)
    table = jnp.cos(jnp.pi * order * ((lane_z % 64).astype(F32) + 0.5) / LZ)
    table = jnp.where(mode // 64 == lane_z // 64, table, 0.0)

    def step(i, carry):
        scaled = base_ref[...] * xrow_ref[pl.ds(i, 1), :]
        log = jnp.dot(scaled, table, precision=lax.Precision.HIGHEST, preferred_element_type=F32)
        xg = start_x + i
        live = inside_y & (xg >= 0) & (xg < NX)
        out_ref[i] = jnp.where(live, 0.5 * jnp.exp(log), 0.0)
        return carry

    lax.fori_loop(0, EXT, step, 0)


def rel(h):
    return jnp.exp(jnp.minimum(h, 0.0))


def sweep_kernel(
    ht_ref, st_ref, nlo_ref, nhi_ref, elo_ref, ehi_ref, cond_ref,
    heads_ref, table_ref,
    ha, hb, ka, kb, sto_ref, src_ref, count_ref, mask_ref,
):
    east = lax.axis_index("east")
    north = lax.axis_index("north")
    low = lanes((8, 128)) < 64
    has_south, has_north = north > 0, north < 15
    has_west, has_east = east > 0, east < 15
    lane = lanes((ROWS, 128))
    row = lax.broadcasted_iota(jnp.int32, (ROWS, 128), 0)
    y = north * CY - 8 + row + (lane // 64) * HALF
    z = lane % 64
    one = lambda c: c.astype(F32)
    count_ref[...] = one(y > 0) + one(y < NY - 1) + one(z > 0) + one(z < LZ - 1)
    mask_ref[...] = one((y >= 0) & (y < NY))
    zl = lanes((8, 128)) % 64
    up_mask = one(zl < LZ - 1)
    down_mask = one(zl > 0)
    gravity = up_mask - down_mask
    zero = jnp.zeros((8, 128), F32)
    for buf in (ha, hb, ka, kb):
        for i in range(EXT):
            buf[i, 0:8] = zero
            buf[i, PAD - 8 : PAD] = zero

    def start(xi, h, s, nlo, nhi, with_source):
        nlo = jnp.where(has_south, nlo, 0.0)
        nhi = jnp.where(has_north, nhi, 0.0)
        pieces = [(0, jnp.where(low, nlo, swap(h[HALF - 8 :])))]
        pieces += [(8 + r, h[r : r + 8]) for r in range(0, HALF, 8)]
        pieces += [(ROWS - 8, swap(jnp.where(low, nhi, h[:8])))]
        if with_source:
            sources = [swap(jnp.where(low, s[HALF - 8 :], nlo))]
            sources += [s[r : r + 8] for r in range(0, HALF, 8)]
            sources += [jnp.where(low, swap(s[:8]), nhi)]
        for n, (r, piece) in enumerate(pieces):
            relative = rel(piece)
            ha[xi, 8 + r : 16 + r] = piece
            ka[xi, 8 + r : 16 + r] = cond_ref[xi, r : r + 8] * relative
            if with_source:
                sto = 0.5 + 0.5 * relative
                sto_ref[xi, r : r + 8] = sto
                src_ref[xi, r : r + 8] = sto * piece + sources[n]

    def own(x, carry):
        start(x + WIDE, ht_ref[x], st_ref[x], nlo_ref[x], nhi_ref[x], True)
        return carry

    lax.fori_loop(0, CX, own, 0)
    for ref, valid, first, flip in ((elo_ref, has_west, 0, 0), (ehi_ref, has_east, EXT - WIDE, 1)):
        for i in range(WIDE):
            h = jnp.where(valid, ref[i * HALF : (i + 1) * HALF], 0.0)
            j = i if flip else i - 1
            if 0 <= j < NSIDE:
                s_at = WIDE * HALF + j * HALF
                c_at = (WIDE + NSIDE) * HALF + j * 8
                s = jnp.where(valid, ref[s_at : s_at + HALF], 0.0)
                nlo = jnp.where(valid, ref[c_at : c_at + 8], 0.0)
                nhi = jnp.where(valid, ref[c_at + NSIDE * 8 : c_at + NSIDE * 8 + 8], 0.0)
                start(first + i, h, s, nlo, nhi, True)
            else:
                start(first + i, h, None, zero, zero, False)

    hin, kin, hout, kout = ha, ka, hb, kb
    for number in range(1, ITERS + 1):

        def sweep(xi, carry, hin=hin, kin=kin, hout=hout, kout=kout):
            xg = east * CX - WIDE + xi
            along_x = one(xg > 0) + one(xg < NX - 1)
            in_x = one((xg >= 0) & (xg < NX))
            for r in range(0, ROWS, 8):
                a = r + 8
                h, k = hin[xi, a : a + 8], kin[xi, a : a + 8]
                hu = pltpu.roll(h, 127, 1) * up_mask
                ku = pltpu.roll(k, 127, 1) * up_mask
                hd = pltpu.roll(h, 1, 1) * down_mask
                kd = pltpu.roll(k, 1, 1) * down_mask
                hn, kn = hin[xi, a + 1 : a + 9], kin[xi, a + 1 : a + 9]
                hs, ks = hin[xi, a - 1 : a + 7], kin[xi, a - 1 : a + 7]
                he, ke = hin[xi + 1, a : a + 8], kin[xi + 1, a : a + 8]
                hw, kw = hin[xi - 1, a : a + 8], kin[xi - 1, a : a + 8]
                sum_h = ((hu + hd) + (hn + hs)) + ((he + hw) + gravity)
                sum_k = ((ku + kd) + (kn + ks)) + (ke + kw)
                flux = ((ku * hu + kd * hd) + (kn * hn + ks * hs)) + (ke * he + kw * hw)
                top = (src_ref[xi, r : r + 8] + k * sum_h) + (flux + (ku - kd))
                below = (count_ref[r : r + 8] + along_x) * k + (sto_ref[xi, r : r + 8] + sum_k)
                inv = pl.reciprocal(below, approx=True)
                inv = inv * (2.0 - below * inv)
                inv = inv * (2.0 - below * inv)
                new = top * inv * in_x
                if r == 0 or r == ROWS - 8:
                    new = new * mask_ref[r : r + 8]
                hout[xi, a : a + 8] = new
                kout[xi, a : a + 8] = cond_ref[xi, r : r + 8] * rel(new)
            return carry

        lax.fori_loop(number, EXT - number, sweep, 0)
        hin, kin, hout, kout = hout, kout, hin, kin

    up2, down2 = up_mask, down_mask
    up2 = jnp.concatenate([up_mask, up_mask], axis=0)
    down2 = jnp.concatenate([down_mask, down_mask], axis=0)

    def velocity(x, carry):
        xi = x + WIDE
        for r in range(0, HALF, 16):
            a = r + 16
            h, k = hin[xi, a : a + 16], kin[xi, a : a + 16]
            heads_ref[x, r : r + 16] = h
            hu = pltpu.roll(h, 127, 1) * up2
            hd = pltpu.roll(h, 1, 1) * down2
            flow_x = -k * (hin[xi + 1, a : a + 16] - hin[xi - 1, a : a + 16])
            flow_y = -k * (hin[xi, a + 1 : a + 17] - hin[xi, a - 1 : a + 15])
            flow_z = -k * ((hu - hd) + 2.0)
            for c, flow in enumerate((flow_x, flow_y, flow_z)):
                big = flow.astype(jnp.bfloat16)
                at = pl.ds(pl.multiple_of(c * CX * HALF + x * HALF + r, 16), 16)
                table_ref[at, 0:128] = big
                table_ref[at, 128:256] = (flow - big.astype(F32)).astype(jnp.bfloat16)
        return carry

    lax.fori_loop(0, CX, velocity, 0)


def onehot_pair(index):
    hot = lax.broadcasted_iota(jnp.int32, (128, index.shape[1]), 0) == index
    hot = jnp.where(hot, 1.0, 0.0).astype(jnp.bfloat16)
    return jnp.concatenate([hot, hot], axis=0)


def choose(get, first, count, bits):
    if count == 1:
        return get(first)
    level = count.bit_length() - 2
    half = count // 2
    low = choose(get, first, half, bits)
    high = choose(get, first + half, half, bits)
    return jnp.where(bits[level], high, low)


BLOCK = 256


def sample_kernel(table_ref, cell_ref, rec_ref, couple_ref, list_ref, count_ref, moved_ref, send_ref, pick_ref):
    def block(n, carry):
        cell = jnp.concatenate([cell_ref[pl.ds(n * 2, 1), :], cell_ref[pl.ds(n * 2 + 1, 1), :]], axis=1)
        layer, i, j = cell >> 11, (cell >> 7) & 15, cell & 127
        lane = (j >> 6) * 64 + layer
        row = i * 64 + (j & 63)
        got = jnp.dot(table_ref[...], onehot_pair(lane), preferred_element_type=F32)
        row8 = jnp.broadcast_to(row, (8, BLOCK))
        bits = [(row8 & (8 << b)) != 0 for b in range(7)]
        mine = lax.broadcasted_iota(jnp.int32, (8, BLOCK), 0) == (row8 & 7)
        at = pl.ds(pl.multiple_of(n * BLOCK, BLOCK), BLOCK)
        total = rec_ref[:, at]
        for c in range(3):
            picked = choose(lambda g: got[c * 1024 + g * 8 : c * 1024 + g * 8 + 8], 0, 128, bits)
            sampled = jnp.sum(jnp.where(mine, picked, 0.0), axis=0, keepdims=True)
            weight = couple_ref[c * 32 : (c + 1) * 32, :]
            total = total + jnp.concatenate([weight, weight], axis=1) * sampled
        moved_ref[:, at] = total
        for half in range(2):
            part = total[:, half * 128 : (half + 1) * 128]
            big = part.astype(jnp.bfloat16)
            rows = pl.ds(pl.multiple_of((n * 2 + half) * 32, 32), 32)
            pick_ref[rows, 0:128] = big
            pick_ref[rows, 128:256] = (part - big.astype(F32)).astype(jnp.bfloat16)
        return carry

    lax.fori_loop(0, 4096 // BLOCK, block, 0)
    for d in range(4):
        for part in range(2):
            index = list_ref[d : d + 1, part * BLOCK : (part + 1) * BLOCK]
            got = jnp.dot(pick_ref[...], onehot_pair(index & 127), preferred_element_type=F32)
            block_of = jnp.broadcast_to(index >> 7, (32, BLOCK))
            bits = [(block_of & (1 << b)) != 0 for b in range(5)]
            picked = choose(lambda g: got[g * 32 : (g + 1) * 32], 0, 32, bits)
            live = lanes((32, BLOCK)) + part * BLOCK < count_ref[d, 0]
            send_ref[d, :, part * BLOCK : (part + 1) * BLOCK] = jnp.where(live, picked, 0.0)


def back_kernel(ht_ref, out_ref):
    for x in range(CX):
        t = ht_ref[x].T
        out_ref[pl.ds(x, LZ, stride=CX), :] = jnp.concatenate([t[:LZ], t[LZ:]], axis=1)


def arrive_kernel(a_ref, b_ref, c_ref, d_ref, out_ref):
    east, north = lax.axis_index("east"), lax.axis_index("north")
    for d, (ref, valid) in enumerate(
        ((a_ref, east > 0), (b_ref, east < 15), (c_ref, north > 0), (d_ref, north < 15))
    ):
        out_ref[d] = jnp.where(valid, ref[...], 0.0)


def call(kernel, outs, ins, scratch=(), limit=None, specs=None, cost=None):
    params = {} if limit is None else dict(compiler_params=pltpu.CompilerParams(vmem_limit_bytes=limit))
    return pl.pallas_call(
        kernel,
        out_shape=[jax.ShapeDtypeStruct(s, t) for s, t in outs],
        in_specs=specs or [VMEM] * len(ins),
        out_specs=[VMEM] * len(outs),
        scratch_shapes=list(scratch),
        cost_estimate=cost,
        **params,
    )(*ins)


def ring(value, axis, steps):
    count = lax.axis_size(axis)
    return lax.ppermute(value, axis, [(i, (i + steps) % count) for i in range(count)])


def mode_weights(mode_coeffs):
    order = jnp.arange(8).astype(F32)
    spectrum = 1.0 / (
        1.0 + (order[:, None, None] ** 2 + order[None, :, None] ** 2 + order[None, None, :] ** 2) / 4.0
    )
    return mode_coeffs * jnp.sqrt(spectrum) * (1.0 / jnp.sqrt(jnp.sum(spectrum)))


def on_device(head_old, source, mode_coeffs, records, cell_index, coupling, send_list, send_count):
    flat = (LZ * CX, CY)
    tile = ((CX, HALF, 128), F32)
    side = ((CX, 8, 128), F32)
    ht, st, n_up, n_down = call(
        turn_kernel, [tile, tile, side, side], [head_old.reshape(flat), source.reshape(flat)]
    )
    nlo = ring(n_up, "north", 1)
    nhi = ring(n_down, "north", -1)
    edge = ((ESEND, 128), F32)
    e_up, e_down = call(pack_kernel, [edge, edge], [ht, st, nlo, nhi])
    elo = ring(e_up, "east", 1)
    ehi = ring(e_down, "east", -1)
    weights = jnp.transpose(mode_weights(mode_coeffs), (2, 0, 1)).reshape(8, 64)
    weights = jnp.concatenate([weights, weights], axis=1)
    (cond,) = call(
        cond_kernel,
        [((EXT, ROWS, 128), F32)],
        [weights],
        [pltpu.VMEM((ROWS, 128), F32), pltpu.VMEM((32, 128), F32)],
    )
    buf = pltpu.VMEM((EXT, PAD, 128), F32)
    ext = pltpu.VMEM((EXT, ROWS, 128), F32)
    plane = pltpu.VMEM((ROWS, 128), F32)
    heads, table = call(
        sweep_kernel,
        [tile, ((3 * CX * HALF, 256), jnp.bfloat16)],
        [ht, st, nlo, nhi, elo, ehi, cond],
        [buf, buf, buf, buf, ext, ext, plane, plane],
        limit=48 * 2**20,
    )
    couple = jnp.broadcast_to((STEP * coupling)[:, :, None], (3, 32, 128)).reshape(96, 128)
    moved, buffers = call(
        sample_kernel,
        [((32, 4096), F32), ((4, 32, 512), F32)],
        [table, cell_index.reshape(32, 128), records, couple, send_list, send_count],
        [pltpu.VMEM((1024, 256), jnp.bfloat16)],
        limit=48 * 2**20,
        specs=[VMEM] * 5 + [SMEM],
    )
    came = [
        ring(buffers[0], "east", 1),
        ring(buffers[1], "east", -1),
        ring(buffers[2], "north", 1),
        ring(buffers[3], "north", -1),
    ]
    (heads_out,) = call(back_kernel, [(flat, F32)], [heads])
    (arrivals,) = call(arrive_kernel, [((4, 32, 512), F32)], came)
    return (heads_out.reshape(LZ, CX, CY), moved, arrivals)


def solution(mesh):
    return jax.shard_map(
        on_device,
        mesh=mesh,
        in_specs=(
            P(None, "east", "north"),
            P(None, "east", "north"),
            P(),
            P(None, ("east", "north")),
            P(("east", "north")),
            P(),
            P(None, ("east", "north")),
            P(None, ("east", "north")),
        ),
        out_specs=(
            P(None, "east", "north"),
            P(None, ("east", "north")),
            P(None, None, ("east", "north")),
        ),
        check_vma=False,
    )
```

```python
import functools

import jax
import jax.numpy as jnp
from jax import lax
from jax.experimental import pallas as pl
from jax.experimental.pallas import tpu as pltpu
from jax.sharding import PartitionSpec as P

ITERS = 4
LZ, CX, CY = 64, 16, 128
HALF = CY // 2
WIDE = ITERS + 1
EXT = CX + 2 * WIDE
ROWS = HALF + 16
PAD = ROWS + 16
NX, NY = 256, 2048
NSIDE = WIDE - 1
ESEND = (WIDE + NSIDE) * HALF + NSIDE * 8
STEP = 0.25
F32 = jnp.float32
VMEM = pl.BlockSpec(memory_space=pltpu.VMEM)
SMEM = pl.BlockSpec(memory_space=pltpu.SMEM)


def lanes(shape):
    return lax.broadcasted_iota(jnp.int32, shape, len(shape) - 1)


def swap(v):
    return pltpu.roll(v, 64, 1)


def turn_kernel(h_ref, s_ref, ht_ref, st_ref, nlo_ref, nhi_ref):
    low = lanes((8, 128)) < 64

    def turned(ref, x):
        t = ref[pl.ds(x, LZ, stride=CX), :].T
        return jnp.concatenate([t[:HALF], t[HALF:]], axis=1)

    for x in range(CX):
        h, s = turned(h_ref, x), turned(s_ref, x)
        ht_ref[x] = h
        st_ref[x] = s
        nlo_ref[x] = jnp.where(low, swap(h[HALF - 8 :]), s[HALF - 8 :])
        nhi_ref[x] = jnp.where(low, h[:8], swap(s[:8]))


def pack_kernel(ht_ref, st_ref, nlo_ref, nhi_ref, elo_ref, ehi_ref):
    upper = lax.broadcasted_iota(jnp.int32, (8, 128), 0) < 4
    for ref, at, at_s in ((elo_ref, CX - WIDE, CX - NSIDE), (ehi_ref, 0, 0)):
        row = 0
        for source, start, count in ((ht_ref, at, WIDE), (st_ref, at_s, NSIDE)):
            for i in range(count):
                ref[row : row + HALF] = source[start + i]
                row += HALF
        for i in range(NSIDE):
            ref[row : row + 8] = jnp.where(upper, nhi_ref[at_s + i], nlo_ref[at_s + i])
            row += 8


def cond_kernel(w_ref, out_ref, base_ref, xrow_ref):
    start_x = lax.axis_index("east") * CX - WIDE
    start_y = lax.axis_index("north") * CY - 8
    lane = lanes((ROWS, 128))
    row = lax.broadcasted_iota(jnp.int32, (ROWS, 128), 0)
    y = start_y + row + (lane // 64) * HALF
    inside_y = (y >= 0) & (y < NY)
    coord = y.astype(F32) + 0.5
    base = jnp.broadcast_to(w_ref[0:1, :], (ROWS, 128))
    for b in range(1, 8):
        base = base + w_ref[b : b + 1, :] * jnp.cos(jnp.pi * float(b) * coord / NY)
    base_ref[...] = base
    lane_x = lanes((32, 128))
    x = start_x + lax.broadcasted_iota(jnp.int32, (32, 128), 0)
    order = (lane_x % 8).astype(F32)
    xrow_ref[...] = jnp.cos(jnp.pi * order * (x.astype(F32) + 0.5) / NX)
    lane_z = lanes((128, 128))
    mode = lax.broadcasted_iota(jnp.int32, (128, 128), 0)
    order = ((mode % 64) // 8).astype(F32)
    table = jnp.cos(jnp.pi * order * ((lane_z % 64).astype(F32) + 0.5) / LZ)
    table = jnp.where(mode // 64 == lane_z // 64, table, 0.0)

    def step(i, carry):
        scaled = base_ref[...] * xrow_ref[pl.ds(i, 1), :]
        log = jnp.dot(scaled, table, precision=lax.Precision.HIGHEST, preferred_element_type=F32)
        xg = start_x + i
        live = inside_y & (xg >= 0) & (xg < NX)
        out_ref[i] = jnp.where(live, 0.5 * jnp.exp(log), 0.0)
        return carry

    lax.fori_loop(0, EXT, step, 0)


def rel(h):
    return jnp.exp(jnp.minimum(h, 0.0))


def one(condition):
    return condition.astype(F32)


def edges():
    z = lanes((8, 128)) % 64
    return one(z < LZ - 1), one(z > 0)


def grid_tables(count_ref, mask_ref):
    north = lax.axis_index("north")
    lane = lanes((ROWS, 128))
    y = north * CY - 8 + lax.broadcasted_iota(jnp.int32, (ROWS, 128), 0) + (lane // 64) * HALF
    z = lane % 64
    count_ref[...] = one(y > 0) + one(y < NY - 1) + one(z > 0) + one(z < LZ - 1)
    mask_ref[...] = one((y >= 0) & (y < NY))


def clear_pads(refs):
    zero = jnp.zeros((8, 128), F32)
    for ref in refs:
        for i in range(ref.shape[0]):
            ref[i, 0:8] = zero
            ref[i, PAD - 8 : PAD] = zero


def start_row(at, h, s, nlo, nhi, cond, ha, ka, sto_ref, src_ref):
    low = lanes((8, 128)) < 64
    north = lax.axis_index("north")
    nlo = jnp.where(north > 0, nlo, 0.0)
    nhi = jnp.where(north < 15, nhi, 0.0)
    pieces = [(0, jnp.where(low, nlo, swap(h[HALF - 8 :])))]
    pieces += [(8 + r, h[r : r + 8]) for r in range(0, HALF, 8)]
    pieces += [(ROWS - 8, swap(jnp.where(low, nhi, h[:8])))]
    if s is not None:
        sources = [swap(jnp.where(low, s[HALF - 8 :], nlo))]
        sources += [s[r : r + 8] for r in range(0, HALF, 8)]
        sources += [jnp.where(low, swap(s[:8]), nhi)]
    for n, (r, piece) in enumerate(pieces):
        relative = rel(piece)
        ha[at, 8 + r : 16 + r] = piece
        ka[at, 8 + r : 16 + r] = cond(r) * relative
        if s is not None:
            sto = 0.5 + 0.5 * relative
            sto_ref[at, r : r + 8] = sto
            src_ref[at, r : r + 8] = sto * piece + sources[n]


def sweep_row(at, xi, hin, kin, hout, kout, cond_ref, sto_ref, src_ref, count_ref, mask_ref):
    up_mask, down_mask = edges()
    gravity = up_mask - down_mask
    xg = lax.axis_index("east") * CX - WIDE + xi
    along_x = one(xg > 0) + one(xg < NX - 1)
    in_x = one((xg >= 0) & (xg < NX))
    for r in range(0, ROWS, 8):
        a = r + 8
        h, k = hin[at, a : a + 8], kin[at, a : a + 8]
        hu = pltpu.roll(h, 127, 1) * up_mask
        ku = pltpu.roll(k, 127, 1) * up_mask
        hd = pltpu.roll(h, 1, 1) * down_mask
        kd = pltpu.roll(k, 1, 1) * down_mask
        hn, kn = hin[at, a + 1 : a + 9], kin[at, a + 1 : a + 9]
        hs, ks = hin[at, a - 1 : a + 7], kin[at, a - 1 : a + 7]
        he, ke = hin[at + 1, a : a + 8], kin[at + 1, a : a + 8]
        hw, kw = hin[at - 1, a : a + 8], kin[at - 1, a : a + 8]
        sum_h = ((hu + hd) + (hn + hs)) + ((he + hw) + gravity)
        sum_k = ((ku + kd) + (kn + ks)) + (ke + kw)
        flux = ((ku * hu + kd * hd) + (kn * hn + ks * hs)) + (ke * he + kw * hw)
        top = (src_ref[at, r : r + 8] + k * sum_h) + (flux + (ku - kd))
        below = (count_ref[r : r + 8] + along_x) * k + (sto_ref[at, r : r + 8] + sum_k)
        inv = pltpu.reciprocal(below, approx=True)
        inv = inv * (2.0 - below * inv)
        inv = inv * (2.0 - below * inv)
        new = top * inv * in_x
        if r == 0 or r == ROWS - 8:
            new = new * mask_ref[r : r + 8]
        hout[at, a : a + 8] = new
        kout[at, a : a + 8] = cond_ref[xi, r : r + 8] * rel(new)


def inner_kernel(
    ht_ref, st_ref, nlo_ref, nhi_ref, cond_ref, ha, hb, ka, kb, sto_ref, src_ref, count_ref, mask_ref
):
    grid_tables(count_ref, mask_ref)
    clear_pads((ha, hb, ka, kb))

    def own(x, carry):
        cond = lambda r: cond_ref[x + WIDE, r : r + 8]
        start_row(x, ht_ref[x], st_ref[x], nlo_ref[x], nhi_ref[x], cond, ha, ka, sto_ref, src_ref)
        return carry

    lax.fori_loop(0, CX, own, 0)
    hin, kin, hout, kout = ha, ka, hb, kb
    for number in range(1, ITERS + 1):

        def sweep(x, carry, hin=hin, kin=kin, hout=hout, kout=kout):
            sweep_row(x, x + WIDE, hin, kin, hout, kout, cond_ref, sto_ref, src_ref, count_ref, mask_ref)
            return carry

        lax.fori_loop(number, CX - number, sweep, 0)
        hin, kin, hout, kout = hout, kout, hin, kin


def outer_kernel(
    ha0, hb0, ka0, kb0, sto0, src0, elo_ref, ehi_ref, cond_ref,
    heads_ref, table_ref,
    ha, hb, ka, kb, sto_ref, src_ref, count_ref, mask_ref,
):
    east = lax.axis_index("east")
    grid_tables(count_ref, mask_ref)
    clear_pads((ha, hb, ka, kb))

    def keep(x, carry):
        for small, big in ((ha0, ha), (hb0, hb), (ka0, ka), (kb0, kb)):
            big[x + WIDE, 8 : PAD - 8] = small[x, 8 : PAD - 8]
        return carry

    lax.fori_loop(0, CX, keep, 0)
    for small, big in ((sto0, sto_ref), (src0, src_ref)):
        for i in range(ITERS):
            big[WIDE + i] = small[i]
            big[EXT - 1 - WIDE - i] = small[CX - 1 - i]
    zero = jnp.zeros((8, 128), F32)
    for ref, valid, first, flip in ((elo_ref, east > 0, 0, 0), (ehi_ref, east < 15, EXT - WIDE, 1)):
        for i in range(WIDE):
            xi = first + i
            h = jnp.where(valid, ref[i * HALF : (i + 1) * HALF], 0.0)
            s, corner = None, zero
            j = i if flip else i - 1
            if 0 <= j < NSIDE:
                s_at = (WIDE + j) * HALF
                c_at = (WIDE + NSIDE) * HALF + j * 8
                s = jnp.where(valid, ref[s_at : s_at + HALF], 0.0)
                corner = jnp.where(valid, ref[c_at : c_at + 8], 0.0)
            cond = lambda r, xi=xi: cond_ref[xi, r : r + 8]
            start_row(xi, h, s, corner, corner, cond, ha, ka, sto_ref, src_ref)

    hin, kin, hout, kout = ha, ka, hb, kb
    for number in range(1, ITERS + 1):

        def sweep(i, carry, number=number, hin=hin, kin=kin, hout=hout, kout=kout):
            xi = number + i + jnp.where(i < WIDE, 0, EXT - 2 * WIDE - 2 * number)
            sweep_row(xi, xi, hin, kin, hout, kout, cond_ref, sto_ref, src_ref, count_ref, mask_ref)
            return carry

        lax.fori_loop(0, 2 * WIDE, sweep, 0)
        hin, kin, hout, kout = hout, kout, hin, kin

    up_mask, down_mask = edges()
    up2 = jnp.concatenate([up_mask, up_mask], axis=0)
    down2 = jnp.concatenate([down_mask, down_mask], axis=0)

    def velocity(x, carry):
        xi = x + WIDE
        for r in range(0, HALF, 16):
            a = r + 16
            h, k = hin[xi, a : a + 16], kin[xi, a : a + 16]
            heads_ref[x, r : r + 16] = h
            hu = pltpu.roll(h, 127, 1) * up2
            hd = pltpu.roll(h, 1, 1) * down2
            flow_x = -k * (hin[xi + 1, a : a + 16] - hin[xi - 1, a : a + 16])
            flow_y = -k * (hin[xi, a + 1 : a + 17] - hin[xi, a - 1 : a + 15])
            flow_z = -k * ((hu - hd) + 2.0)
            for c, flow in enumerate((flow_x, flow_y, flow_z)):
                big = flow.astype(jnp.bfloat16)
                at = pl.ds(pl.multiple_of(c * CX * HALF + x * HALF + r, 16), 16)
                table_ref[at, 0:128] = big
                table_ref[at, 128:256] = (flow - big.astype(F32)).astype(jnp.bfloat16)
        return carry

    lax.fori_loop(0, CX, velocity, 0)


def onehot_pair(index):
    hot = lax.broadcasted_iota(jnp.int32, (128, index.shape[1]), 0) == index
    hot = jnp.where(hot, 1.0, 0.0).astype(jnp.bfloat16)
    return jnp.concatenate([hot, hot], axis=0)


def choose(get, first, count, bits):
    if count == 1:
        return get(first)
    level = count.bit_length() - 2
    half = count // 2
    low = choose(get, first, half, bits)
    high = choose(get, first + half, half, bits)
    return jnp.where(bits[level], high, low)


BLOCK = 256


def sample_kernel(table_ref, cell_ref, rec_ref, couple_ref, list_ref, count_ref, moved_ref, send_ref, pick_ref):
    def block(n, carry):
        cell = jnp.concatenate([cell_ref[pl.ds(n * 2, 1), :], cell_ref[pl.ds(n * 2 + 1, 1), :]], axis=1)
        layer, i, j = cell >> 11, (cell >> 7) & 15, cell & 127
        lane = (j >> 6) * 64 + layer
        row = i * 64 + (j & 63)
        got = jnp.dot(table_ref[...], onehot_pair(lane), preferred_element_type=F32)
        row8 = jnp.broadcast_to(row, (8, BLOCK))
        bits = [(row8 & (8 << b)) != 0 for b in range(7)]
        mine = lax.broadcasted_iota(jnp.int32, (8, BLOCK), 0) == (row8 & 7)
        at = pl.ds(pl.multiple_of(n * BLOCK, BLOCK), BLOCK)
        total = rec_ref[:, at]
        for c in range(3):
            picked = choose(lambda g: got[c * 1024 + g * 8 : c * 1024 + g * 8 + 8], 0, 128, bits)
            sampled = jnp.sum(jnp.where(mine, picked, 0.0), axis=0, keepdims=True)
            weight = couple_ref[c * 32 : (c + 1) * 32, :]
            total = total + jnp.concatenate([weight, weight], axis=1) * sampled
        moved_ref[:, at] = total
        for half in range(2):
            part = total[:, half * 128 : (half + 1) * 128]
            big = part.astype(jnp.bfloat16)
            rows = pl.ds(pl.multiple_of((n * 2 + half) * 32, 32), 32)
            pick_ref[rows, 0:128] = big
            pick_ref[rows, 128:256] = (part - big.astype(F32)).astype(jnp.bfloat16)
        return carry

    lax.fori_loop(0, 4096 // BLOCK, block, 0)
    for d in range(4):
        for part in range(2):
            index = list_ref[d : d + 1, part * BLOCK : (part + 1) * BLOCK]
            got = jnp.dot(pick_ref[...], onehot_pair(index & 127), preferred_element_type=F32)
            block_of = jnp.broadcast_to(index >> 7, (32, BLOCK))
            bits = [(block_of & (1 << b)) != 0 for b in range(5)]
            picked = choose(lambda g: got[g * 32 : (g + 1) * 32], 0, 32, bits)
            live = lanes((32, BLOCK)) + part * BLOCK < count_ref[d, 0]
            send_ref[d, :, part * BLOCK : (part + 1) * BLOCK] = jnp.where(live, picked, 0.0)


def back_kernel(ht_ref, out_ref):
    for x in range(CX):
        t = ht_ref[x].T
        out_ref[pl.ds(x, LZ, stride=CX), :] = jnp.concatenate([t[:LZ], t[LZ:]], axis=1)


def arrive_kernel(a_ref, b_ref, c_ref, d_ref, out_ref):
    east, north = lax.axis_index("east"), lax.axis_index("north")
    for d, (ref, valid) in enumerate(
        ((a_ref, east > 0), (b_ref, east < 15), (c_ref, north > 0), (d_ref, north < 15))
    ):
        out_ref[d] = jnp.where(valid, ref[...], 0.0)


def call(kernel, outs, ins, scratch=(), limit=6, specs=None):
    return pl.pallas_call(
        kernel,
        out_shape=[jax.ShapeDtypeStruct(s, t) for s, t in outs],
        in_specs=specs or [VMEM] * len(ins),
        out_specs=[VMEM] * len(outs),
        scratch_shapes=list(scratch),
        compiler_params=pltpu.CompilerParams(vmem_limit_bytes=limit * 2**20),
    )(*ins)


def ring(value, axis, steps):
    count = lax.axis_size(axis)
    return lax.ppermute(value, axis, [(i, (i + steps) % count) for i in range(count)])


def mode_weights(mode_coeffs):
    order = jnp.arange(8).astype(F32)
    spectrum = 1.0 / (
        1.0 + (order[:, None, None] ** 2 + order[None, :, None] ** 2 + order[None, None, :] ** 2) / 4.0
    )
    return mode_coeffs * jnp.sqrt(spectrum) * (1.0 / jnp.sqrt(jnp.sum(spectrum)))


def on_device(head_old, source, mode_coeffs, records, cell_index, coupling, send_list, send_count):
    flat = (LZ * CX, CY)
    tile = ((CX, HALF, 128), F32)
    side = ((CX, 8, 128), F32)
    ht, st, n_up, n_down = call(
        turn_kernel, [tile, tile, side, side], [head_old.reshape(flat), source.reshape(flat)]
    )
    nlo = ring(n_up, "north", 1)
    nhi = ring(n_down, "north", -1)
    edge = ((ESEND, 128), F32)
    e_up, e_down = call(pack_kernel, [edge, edge], [ht, st, nlo, nhi])
    elo = ring(e_up, "east", 1)
    ehi = ring(e_down, "east", -1)
    weights = jnp.transpose(mode_weights(mode_coeffs), (2, 0, 1)).reshape(8, 64)
    weights = jnp.concatenate([weights, weights], axis=1)
    (cond,) = call(
        cond_kernel,
        [((EXT, ROWS, 128), F32)],
        [weights],
        [pltpu.VMEM((ROWS, 128), F32), pltpu.VMEM((32, 128), F32)],
    )
    plane = pltpu.VMEM((ROWS, 128), F32)
    level = ((CX, PAD, 128), F32)
    base = ((CX, ROWS, 128), F32)
    inner = call(
        inner_kernel, [level] * 4 + [base] * 2, [ht, st, nlo, nhi, cond], [plane, plane], limit=12
    )
    buf = pltpu.VMEM((EXT, PAD, 128), F32)
    ext = pltpu.VMEM((EXT, ROWS, 128), F32)
    heads, table = call(
        outer_kernel,
        [tile, ((3 * CX * HALF, 256), jnp.bfloat16)],
        list(inner) + [elo, ehi, cond],
        [buf, buf, buf, buf, ext, ext, plane, plane],
        limit=20,
    )
    couple = jnp.broadcast_to((STEP * coupling)[:, :, None], (3, 32, 128)).reshape(96, 128)
    moved, buffers = call(
        sample_kernel,
        [((32, 4096), F32), ((4, 32, 512), F32)],
        [table, cell_index.reshape(32, 128), records, couple, send_list, send_count],
        [pltpu.VMEM((1024, 256), jnp.bfloat16)],
        limit=24,
        specs=[VMEM] * 5 + [SMEM],
    )
    came = [
        ring(buffers[0], "east", 1),
        ring(buffers[1], "east", -1),
        ring(buffers[2], "north", 1),
        ring(buffers[3], "north", -1),
    ]
    (heads_out,) = call(back_kernel, [(flat, F32)], [heads])
    (arrivals,) = call(arrive_kernel, [((4, 32, 512), F32)], came)
    return (heads_out.reshape(LZ, CX, CY), moved, arrivals)


def solution(mesh):
    return jax.shard_map(
        on_device,
        mesh=mesh,
        in_specs=(
            P(None, "east", "north"),
            P(None, "east", "north"),
            P(),
            P(None, ("east", "north")),
            P(("east", "north")),
            P(),
            P(None, ("east", "north")),
            P(None, ("east", "north")),
        ),
        out_specs=(
            P(None, "east", "north"),
            P(None, ("east", "north")),
            P(None, None, ("east", "north")),
        ),
        check_vma=False,
    )
```

```python
import jax
import jax.numpy as jnp
from jax import lax
from jax.experimental import pallas as pl
from jax.experimental.pallas import tpu as pltpu
from jax.sharding import PartitionSpec as P

ITERS = 4
LZ, CX, CY = 64, 16, 128
HALF = CY // 2
WIDE = ITERS + 1
EXT = CX + 2 * WIDE
ROWS = HALF + 16
PAD = ROWS + 8
MID = CX - 2 * WIDE
OUT = CX - MID
NX, NY = 256, 2048
NSIDE = WIDE - 1
ESEND = (WIDE + NSIDE) * HALF + NSIDE * 8
STEP = 0.25
F32 = jnp.float32
VMEM = pl.BlockSpec(memory_space=pltpu.VMEM)
SMEM = pl.BlockSpec(memory_space=pltpu.SMEM)


def lanes(shape):
    return lax.broadcasted_iota(jnp.int32, shape, len(shape) - 1)


def swap(v):
    return pltpu.roll(v, 64, 1)


def turned(ref, x):
    t = ref[pl.ds(x, LZ, stride=CX), :].T
    return jnp.concatenate([t[:HALF], t[HALF:]], axis=1)


def turn_kernel(h_ref, ht_ref):
    for x in range(CX):
        ht_ref[x] = turned(h_ref, x)


def turn_source_kernel(s_ref, ht_ref, st_ref, nlo_ref, nhi_ref):
    low = lanes((8, 128)) < 64
    for x in range(CX):
        s = turned(s_ref, x)
        st_ref[x] = s
        nlo_ref[x] = jnp.where(low, swap(ht_ref[x, HALF - 8 :]), s[HALF - 8 :])
        nhi_ref[x] = jnp.where(low, ht_ref[x, :8], swap(s[:8]))


def pack_kernel(ht_ref, st_ref, nlo_ref, nhi_ref, elo_ref, ehi_ref):
    upper = lax.broadcasted_iota(jnp.int32, (8, 128), 0) < 4
    for ref, at, at_s in ((elo_ref, CX - WIDE, CX - NSIDE), (ehi_ref, 0, 0)):
        row = 0
        for source, start, count in ((ht_ref, at, WIDE), (st_ref, at_s, NSIDE)):
            for i in range(count):
                ref[row : row + HALF] = source[start + i]
                row += HALF
        for i in range(NSIDE):
            ref[row : row + 8] = jnp.where(upper, nhi_ref[at_s + i], nlo_ref[at_s + i])
            row += 8


def cond_kernel(modes_ref, out_ref, work_ref, xrow_ref):
    start_x = lax.axis_index("east") * CX - WIDE
    start_y = lax.axis_index("north") * CY - 8
    exact = dict(precision=lax.Precision.HIGHEST, preferred_element_type=F32)
    ca = lax.broadcasted_iota(jnp.int32, (64, 8), 0)
    order_c, order_a, order_b = (ca // 8).astype(F32), (ca % 8).astype(F32), lanes((64, 8)).astype(F32)
    spectrum = 1.0 / (1.0 + (order_c * order_c + order_a * order_a + order_b * order_b) / 4.0)
    total = jnp.sum(jnp.sum(spectrum, axis=1, keepdims=True), axis=0, keepdims=True)
    weights = modes_ref[...] * jnp.sqrt(spectrum) * (1.0 / jnp.sqrt(total))
    row = lax.broadcasted_iota(jnp.int32, (ROWS, 8), 0)
    order = lanes((ROWS, 8)).astype(F32)
    halves = []
    for half in range(2):
        coord = (start_y + half * HALF + row).astype(F32) + 0.5
        table = jnp.cos(jnp.pi * order * coord / NY)
        halves.append(lax.dot_general(table, weights, (((1,), (1,)), ((), ())), **exact))
    base = jnp.concatenate(halves, axis=1)
    x = start_x + lax.broadcasted_iota(jnp.int32, (32, 128), 0)
    order = (lanes((32, 128)) % 8).astype(F32)
    xrow_ref[...] = jnp.cos(jnp.pi * order * (x.astype(F32) + 0.5) / NX)
    lane_z = lanes((128, 128))
    mode = lax.broadcasted_iota(jnp.int32, (128, 128), 0)
    order = ((mode % 64) // 8).astype(F32)
    table = jnp.cos(jnp.pi * order * ((lane_z % 64).astype(F32) + 0.5) / LZ)
    table = jnp.where(mode // 64 == lane_z // 64, table, 0.0)
    lane = lanes((ROWS, 128))
    y = start_y + lax.broadcasted_iota(jnp.int32, (ROWS, 128), 0) + (lane // 64) * HALF
    inside_y = one((y >= 0) & (y < NY))
    for first in range(0, EXT, EXT // 2):
        for i in range(EXT // 2):
            work_ref[i * ROWS : (i + 1) * ROWS] = base * xrow_ref[first + i : first + i + 1, :]
        log = jnp.dot(work_ref[...], table, **exact)
        for i in range(EXT // 2):
            xg = start_x + first + i
            live = inside_y * one((xg >= 0) & (xg < NX))
            value = jnp.exp(log[i * ROWS : (i + 1) * ROWS])
            out_ref[first + i] = jnp.where(live > 0.0, 0.5 * value, 0.0)


def rel(h):
    return jnp.exp(jnp.minimum(h, 0.0))


def one(condition):
    return condition.astype(F32)


def split(ref, at, value):
    big = value.astype(jnp.bfloat16)
    ref[at, 0:128] = big
    ref[at, 128:256] = (value - big.astype(F32)).astype(jnp.bfloat16)


def edges():
    z = lanes((8, 128)) % 64
    return one(z < LZ - 1), one(z > 0)


def grid_tables(count_ref, mask_ref):
    north = lax.axis_index("north")
    lane = lanes((ROWS, 128))
    y = north * CY - 8 + lax.broadcasted_iota(jnp.int32, (ROWS, 128), 0) + (lane // 64) * HALF
    z = lane % 64
    count_ref[...] = one(y > 0) + one(y < NY - 1) + one(z > 0) + one(z < LZ - 1)
    mask_ref[...] = one((y >= 0) & (y < NY))


def clear_pads(refs):
    zero = jnp.zeros((8, 128), F32)
    for ref in refs:
        for i in range(ref.shape[0]):
            ref[i, 0:8] = zero
            ref[i, PAD - 8 : PAD] = zero


def start_row(at, h, s, nlo, nhi, cond, ha, ka, sto_ref, src_ref):
    low = lanes((8, 128)) < 64
    north = lax.axis_index("north")
    nlo = jnp.where(north > 0, nlo, 0.0)
    nhi = jnp.where(north < 15, nhi, 0.0)
    pieces = [(0, jnp.where(low, nlo, swap(h[HALF - 8 :])))]
    pieces += [(8 + r, h[r : r + 8]) for r in range(0, HALF, 8)]
    pieces += [(ROWS - 8, swap(jnp.where(low, nhi, h[:8])))]
    if s is not None:
        sources = [swap(jnp.where(low, s[HALF - 8 :], nlo))]
        sources += [s[r : r + 8] for r in range(0, HALF, 8)]
        sources += [jnp.where(low, swap(s[:8]), nhi)]
    for n, (r, piece) in enumerate(pieces):
        relative = rel(piece)
        ha[at, 4 + r : 12 + r] = piece
        ka[at, 4 + r : 12 + r] = cond(r) * relative
        if s is not None:
            sto = 0.5 + 0.5 * relative
            sto_ref[at, r : r + 8] = sto
            src_ref[at, r : r + 8] = sto * piece + sources[n]


def sweep_row(at, xi, hin, kin, hout, kout, cond_ref, sto_ref, src_ref, count_ref, mask_ref):
    up_mask, down_mask = edges()
    gravity = up_mask - down_mask
    xg = lax.axis_index("east") * CX - WIDE + xi
    along_x = one(xg > 0) + one(xg < NX - 1)
    in_x = one((xg >= 0) & (xg < NX))
    for a in range(8, PAD - 8, 8):
        r = a - 4
        h, k = hin[at, a : a + 8], kin[at, a : a + 8]
        hu = pltpu.roll(h, 127, 1) * up_mask
        ku = pltpu.roll(k, 127, 1) * up_mask
        hd = pltpu.roll(h, 1, 1) * down_mask
        kd = pltpu.roll(k, 1, 1) * down_mask
        hn, kn = hin[at, a + 1 : a + 9], kin[at, a + 1 : a + 9]
        hs, ks = hin[at, a - 1 : a + 7], kin[at, a - 1 : a + 7]
        he, ke = hin[at + 1, a : a + 8], kin[at + 1, a : a + 8]
        hw, kw = hin[at - 1, a : a + 8], kin[at - 1, a : a + 8]
        sum_h = ((hu + hd) + (hn + hs)) + ((he + hw) + gravity)
        sum_k = ((ku + kd) + (kn + ks)) + (ke + kw)
        flux = ((ku * hu + kd * hd) + (kn * hn + ks * hs)) + (ke * he + kw * hw)
        top = (src_ref[at, r : r + 8] + k * sum_h) + (flux + (ku - kd))
        below = (count_ref[r : r + 8] + along_x) * k + (sto_ref[at, r : r + 8] + sum_k)
        inv = pltpu.reciprocal(below, approx=True)
        inv = inv * (2.0 - below * inv)
        inv = inv * (2.0 - below * inv)
        new = top * inv * in_x
        if a == 8 or a == PAD - 16:
            new = new * mask_ref[r : r + 8]
        hout[at, a : a + 8] = new
        kout[at, a : a + 8] = cond_ref[xi, r : r + 8] * rel(new)


def velocity_row(at, row, size, h_ref, k_ref, table_ref):
    up_mask, down_mask = edges()
    up_mask = jnp.concatenate([up_mask, up_mask], axis=0)
    down_mask = jnp.concatenate([down_mask, down_mask], axis=0)
    for r in range(0, HALF, 16):
        a = r + 12
        h, k = h_ref[at, a : a + 16], k_ref[at, a : a + 16]
        hu = pltpu.roll(h, 127, 1) * up_mask
        hd = pltpu.roll(h, 1, 1) * down_mask
        flow_x = -k * (h_ref[at + 1, a : a + 16] - h_ref[at - 1, a : a + 16])
        flow_y = -k * (h_ref[at, a + 1 : a + 17] - h_ref[at, a - 1 : a + 15])
        flow_z = -k * ((hu - hd) + 2.0)
        for c, flow in enumerate((flow_x, flow_y, flow_z)):
            split(table_ref, pl.ds(pl.multiple_of(row + c * size + r, 16), 16), flow)


def inner_kernel(
    ht_ref, st_ref, nlo_ref, nhi_ref, cond_ref,
    ha, hb, ka, kb, sto_ref, src_ref, table_ref,
    count_ref, mask_ref,
):
    grid_tables(count_ref, mask_ref)
    clear_pads((hb, kb))

    def own(x, carry):
        cond = lambda r: cond_ref[x + WIDE, r : r + 8]
        start_row(x, ht_ref[x], st_ref[x], nlo_ref[x], nhi_ref[x], cond, ha, ka, sto_ref, src_ref)
        return carry

    lax.fori_loop(0, CX, own, 0)
    hin, kin, hout, kout = ha, ka, hb, kb
    for number in range(1, ITERS + 1):

        def sweep(x, carry, hin=hin, kin=kin, hout=hout, kout=kout):
            sweep_row(x, x + WIDE, hin, kin, hout, kout, cond_ref, sto_ref, src_ref, count_ref, mask_ref)
            return carry

        lax.fori_loop(number, CX - number, sweep, 0)
        hin, kin, hout, kout = hout, kout, hin, kin

    def velocity(i, carry):
        velocity_row(i + WIDE, i * HALF, MID * HALF, hin, kin, table_ref)
        return carry

    lax.fori_loop(0, MID, velocity, 0)


def outer_kernel(
    ha0, hb0, ka0, kb0, sto0, src0, elo_ref, ehi_ref, cond_ref,
    heads_ref, table_ref,
    ha, hb, ka, kb, sto_ref, src_ref, count_ref, mask_ref,
):
    east = lax.axis_index("east")
    grid_tables(count_ref, mask_ref)
    clear_pads((hb, kb))
    for x in range(CX):
        depth = min(x, CX - 1 - x)
        if depth <= WIDE:
            ha[x + WIDE], ka[x + WIDE] = ha0[x], ka0[x]
        if 1 <= depth <= ITERS:
            hb[x + WIDE], kb[x + WIDE] = hb0[x], kb0[x]
    for small, big in ((sto0, sto_ref), (src0, src_ref)):
        for i in range(ITERS):
            big[WIDE + i] = small[i]
            big[EXT - 1 - WIDE - i] = small[CX - 1 - i]
    zero = jnp.zeros((8, 128), F32)
    for ref, valid, first, flip in ((elo_ref, east > 0, 0, 0), (ehi_ref, east < 15, EXT - WIDE, 1)):
        for i in range(WIDE):
            xi = first + i
            h = jnp.where(valid, ref[i * HALF : (i + 1) * HALF], 0.0)
            s, corner = None, zero
            j = i if flip else i - 1
            if 0 <= j < NSIDE:
                s_at = (WIDE + j) * HALF
                c_at = (WIDE + NSIDE) * HALF + j * 8
                s = jnp.where(valid, ref[s_at : s_at + HALF], 0.0)
                corner = jnp.where(valid, ref[c_at : c_at + 8], 0.0)
            cond = lambda r, xi=xi: cond_ref[xi, r : r + 8]
            start_row(xi, h, s, corner, corner, cond, ha, ka, sto_ref, src_ref)

    hin, kin, hout, kout = ha, ka, hb, kb
    for number in range(1, ITERS + 1):

        def sweep(i, carry, number=number, hin=hin, kin=kin, hout=hout, kout=kout):
            xi = number + i + jnp.where(i < WIDE, 0, EXT - 2 * WIDE - 2 * number)
            sweep_row(xi, xi, hin, kin, hout, kout, cond_ref, sto_ref, src_ref, count_ref, mask_ref)
            return carry

        lax.fori_loop(0, 2 * WIDE, sweep, 0)
        hin, kin, hout, kout = hout, kout, hin, kin

    for x in range(CX):
        source, at = (ha0, x) if WIDE <= x < CX - WIDE else (hin, x + WIDE)
        heads_ref[x] = source[at, 12 : 12 + HALF]

    def velocity(i, carry):
        at = i + WIDE + jnp.where(i < WIDE, 0, MID)
        velocity_row(at, i * HALF, OUT * HALF, hin, kin, table_ref)
        return carry

    lax.fori_loop(0, OUT, velocity, 0)


def onehot_pair(index):
    hot = lax.broadcasted_iota(jnp.int32, (128, index.shape[1]), 0) == index
    hot = jnp.where(hot, 1.0, 0.0).astype(jnp.bfloat16)
    return jnp.concatenate([hot, hot], axis=0)


def choose(get, first, count, bits):
    if count == 1:
        return get(first)
    level = (count - 1).bit_length() - 1
    half = 1 << level
    low = choose(get, first, half, bits)
    high = choose(get, first + half, count - half, bits)
    return jnp.where(bits[level], high, low)


BLOCK = 512
PARTS = BLOCK // 128


def read_cells(cell_ref, n):
    cell = jnp.concatenate([cell_ref[pl.ds(n * PARTS + i, 1), :] for i in range(PARTS)], axis=1)
    layer, x, j = cell >> 11, (cell >> 7) & 15, cell & 127
    return x, j & 63, (j >> 6) * 64 + layer


def sampled_at(table_ref, count, place, inner_y, lane):
    got = jnp.dot(table_ref[...], onehot_pair(lane), preferred_element_type=F32)
    row8 = jnp.broadcast_to(place * 64 + inner_y, (8, BLOCK))
    bits = [(row8 & (8 << b)) != 0 for b in range(7)]
    mine = lax.broadcasted_iota(jnp.int32, (8, BLOCK), 0) == (row8 & 7)
    size = count * HALF
    for c in range(3):
        picked = choose(lambda g: got[c * size + g * 8 : c * size + g * 8 + 8], 0, count * 8, bits)
        yield c, jnp.sum(jnp.where(mine, picked, 0.0), axis=0, keepdims=True)


def sample_inner_kernel(table_ref, cell_ref, part_ref):
    def block(n, carry):
        x, inner_y, lane = read_cells(cell_ref, n)
        at = pl.ds(pl.multiple_of(n * BLOCK, BLOCK), BLOCK)
        for c, sampled in sampled_at(table_ref, MID, jnp.clip(x - WIDE, 0, MID - 1), inner_y, lane):
            part_ref[c : c + 1, at] = sampled
        return carry

    lax.fori_loop(0, 4096 // BLOCK, block, 0)


def sample_kernel(
    table_ref, cell_ref, part_ref, rec_ref, couple_ref, list_ref, count_ref, moved_ref, send_ref, pick_ref
):
    def block(n, carry):
        x, inner_y, lane = read_cells(cell_ref, n)
        middle = (x >= WIDE) & (x < CX - WIDE)
        place = jnp.where(x < WIDE, x, jnp.maximum(x - MID, 0))
        at = pl.ds(pl.multiple_of(n * BLOCK, BLOCK), BLOCK)
        total = rec_ref[:, at]
        for c, outer in sampled_at(table_ref, OUT, place, inner_y, lane):
            sampled = jnp.where(middle, part_ref[c : c + 1, at], outer)
            weight = couple_ref[c * 32 : (c + 1) * 32, :]
            total = total + jnp.concatenate([weight] * PARTS, axis=1) * sampled
        moved_ref[:, at] = total
        for i in range(PARTS):
            rows = pl.ds(pl.multiple_of((n * PARTS + i) * 32, 32), 32)
            split(pick_ref, rows, total[:, i * 128 : (i + 1) * 128])
        return carry

    lax.fori_loop(0, 4096 // BLOCK, block, 0)
    for d in range(4):
        index = list_ref[d : d + 1, :]
        got = jnp.dot(pick_ref[...], onehot_pair(index & 127), preferred_element_type=F32)
        block_of = jnp.broadcast_to(index >> 7, (32, BLOCK))
        bits = [(block_of & (1 << b)) != 0 for b in range(5)]
        picked = choose(lambda g: got[g * 32 : (g + 1) * 32], 0, 32, bits)
        live = lanes((32, BLOCK)) < count_ref[d, 0]
        send_ref[d] = jnp.where(live, picked, 0.0)


def back_kernel(ht_ref, out_ref):
    for x in range(CX):
        t = ht_ref[x].T
        out_ref[pl.ds(x, LZ, stride=CX), :] = jnp.concatenate([t[:LZ], t[LZ:]], axis=1)


def arrive_kernel(a_ref, b_ref, c_ref, d_ref, out_ref):
    east, north = lax.axis_index("east"), lax.axis_index("north")
    for d, (ref, valid) in enumerate(
        ((a_ref, east > 0), (b_ref, east < 15), (c_ref, north > 0), (d_ref, north < 15))
    ):
        out_ref[d] = jnp.where(valid, ref[...], 0.0)


def call(kernel, outs, ins, scratch=(), limit=6, specs=None):
    return pl.pallas_call(
        kernel,
        out_shape=[jax.ShapeDtypeStruct(s, t) for s, t in outs],
        in_specs=specs or [VMEM] * len(ins),
        out_specs=[VMEM] * len(outs),
        scratch_shapes=list(scratch),
        compiler_params=pltpu.CompilerParams(vmem_limit_bytes=limit * 2**20),
    )(*ins)


def ring(value, axis, steps):
    count = lax.axis_size(axis)
    return lax.ppermute(value, axis, [(i, (i + steps) % count) for i in range(count)])


def on_device(head_old, source, mode_coeffs, records, cell_index, coupling, send_list, send_count):
    flat = (LZ * CX, CY)
    tile = ((CX, HALF, 128), F32)
    side = ((CX, 8, 128), F32)
    (ht,) = call(turn_kernel, [tile], [head_old.reshape(flat)])
    st, n_up, n_down = call(turn_source_kernel, [tile, side, side], [source.reshape(flat), ht])
    nlo = ring(n_up, "north", 1)
    nhi = ring(n_down, "north", -1)
    edge = ((ESEND, 128), F32)
    e_up, e_down = call(pack_kernel, [edge, edge], [ht, st, nlo, nhi])
    elo = ring(e_up, "east", 1)
    ehi = ring(e_down, "east", -1)
    (cond,) = call(
        cond_kernel,
        [((EXT, ROWS, 128), F32)],
        [mode_coeffs.reshape(64, 8)],
        [pltpu.VMEM((EXT // 2 * ROWS, 128), F32), pltpu.VMEM((32, 128), F32)],
        limit=12,
    )
    plane = pltpu.VMEM((ROWS, 128), F32)
    level = ((CX, PAD, 128), F32)
    base = ((CX, ROWS, 128), F32)
    cells = cell_index.reshape(32, 128)
    *inner, table_mid = call(
        inner_kernel,
        [level] * 4 + [base] * 2 + [((3 * MID * HALF, 256), jnp.bfloat16)],
        [ht, st, nlo, nhi, cond],
        [plane, plane],
        limit=12,
    )
    (part,) = call(sample_inner_kernel, [((8, 4096), F32)], [table_mid, cells], limit=12)
    buf = pltpu.VMEM((EXT, PAD, 128), F32)
    ext = pltpu.VMEM((EXT, ROWS, 128), F32)
    heads, table = call(
        outer_kernel,
        [tile, ((3 * OUT * HALF, 256), jnp.bfloat16)],
        list(inner) + [elo, ehi, cond],
        [buf, buf, buf, buf, ext, ext, plane, plane],
        limit=20,
    )
    couple = jnp.broadcast_to((STEP * coupling)[:, :, None], (3, 32, 128)).reshape(96, 128)
    moved, buffers = call(
        sample_kernel,
        [((32, 4096), F32), ((4, 32, 512), F32)],
        [table, cells, part, records, couple, send_list, send_count],
        [pltpu.VMEM((1024, 256), jnp.bfloat16)],
        limit=24,
        specs=[VMEM] * 6 + [SMEM],
    )
    came = [
        ring(buffers[0], "east", 1),
        ring(buffers[1], "east", -1),
        ring(buffers[2], "north", 1),
        ring(buffers[3], "north", -1),
    ]
    (heads_out,) = call(back_kernel, [(flat, F32)], [heads])
    (arrivals,) = call(arrive_kernel, [((4, 32, 512), F32)], came)
    return (heads_out.reshape(LZ, CX, CY), moved, arrivals)


def solution(mesh):
    return jax.shard_map(
        on_device,
        mesh=mesh,
        in_specs=(
            P(None, "east", "north"),
            P(None, "east", "north"),
            P(),
            P(None, ("east", "north")),
            P(("east", "north")),
            P(),
            P(None, ("east", "north")),
            P(None, ("east", "north")),
        ),
        out_specs=(
            P(None, "east", "north"),
            P(None, ("east", "north")),
            P(None, None, ("east", "north")),
        ),
        check_vma=False,
    )
```

```python
import jax
import jax.numpy as jnp
from jax import lax
from jax.experimental import pallas as pl
from jax.experimental.pallas import tpu as pltpu
from jax.sharding import PartitionSpec as P

ITERS = 4
LZ, CX, CY = 64, 16, 128
HALF = CY // 2
WIDE = ITERS + 1
EXT = CX + 2 * WIDE
ROWS = HALF + 16
PAD = ROWS + 8
MID = CX - 2 * WIDE
OUT = CX - MID
NX, NY = 256, 2048
NSIDE = WIDE - 1
ESEND = (WIDE + NSIDE) * HALF + NSIDE * 8
STEP = 0.25
F32 = jnp.float32
VMEM = pl.BlockSpec(memory_space=pltpu.VMEM)
SMEM = pl.BlockSpec(memory_space=pltpu.SMEM)


def lanes(shape):
    return lax.broadcasted_iota(jnp.int32, shape, len(shape) - 1)


def swap(v):
    return pltpu.roll(v, 64, 1)


def turned(ref, x):
    t = ref[pl.ds(x, LZ, stride=CX), :].T
    return jnp.concatenate([t[:HALF], t[HALF:]], axis=1)


def turn_kernel(h_ref, ht_ref):
    for x in range(CX):
        ht_ref[x] = turned(h_ref, x)


def turn_source_kernel(s_ref, ht_ref, st_ref, nlo_ref, nhi_ref):
    low = lanes((8, 128)) < 64
    for x in range(CX):
        s = turned(s_ref, x)
        st_ref[x] = s
        nlo_ref[x] = jnp.where(low, swap(ht_ref[x, HALF - 8 :]), s[HALF - 8 :])
        nhi_ref[x] = jnp.where(low, ht_ref[x, :8], swap(s[:8]))


def pack_kernel(ht_ref, st_ref, nlo_ref, nhi_ref, elo_ref, ehi_ref):
    upper = lax.broadcasted_iota(jnp.int32, (8, 128), 0) < 4
    for ref, at, at_s in ((elo_ref, CX - WIDE, CX - NSIDE), (ehi_ref, 0, 0)):
        row = 0
        for source, start, count in ((ht_ref, at, WIDE), (st_ref, at_s, NSIDE)):
            for i in range(count):
                ref[row : row + HALF] = source[start + i]
                row += HALF
        for i in range(NSIDE):
            ref[row : row + 8] = jnp.where(upper, nhi_ref[at_s + i], nlo_ref[at_s + i])
            row += 8


def cond_kernel(modes_ref, out_ref, work_ref, xrow_ref):
    start_x = lax.axis_index("east") * CX - WIDE
    start_y = lax.axis_index("north") * CY - 8
    exact = dict(precision=lax.Precision.HIGHEST, preferred_element_type=F32)
    ca = lax.broadcasted_iota(jnp.int32, (64, 8), 0)
    order_c, order_a, order_b = (ca // 8).astype(F32), (ca % 8).astype(F32), lanes((64, 8)).astype(F32)
    spectrum = 1.0 / (1.0 + (order_c * order_c + order_a * order_a + order_b * order_b) / 4.0)
    total = jnp.sum(jnp.sum(spectrum, axis=1, keepdims=True), axis=0, keepdims=True)
    weights = modes_ref[...] * jnp.sqrt(spectrum) * (1.0 / jnp.sqrt(total))
    row = lax.broadcasted_iota(jnp.int32, (ROWS, 8), 0)
    order = lanes((ROWS, 8)).astype(F32)
    halves = []
    for half in range(2):
        coord = (start_y + half * HALF + row).astype(F32) + 0.5
        table = jnp.cos(jnp.pi * order * coord / NY)
        halves.append(lax.dot_general(table, weights, (((1,), (1,)), ((), ())), **exact))
    base = jnp.concatenate(halves, axis=1)
    x = start_x + lax.broadcasted_iota(jnp.int32, (32, 128), 0)
    order = (lanes((32, 128)) % 8).astype(F32)
    xrow_ref[...] = jnp.cos(jnp.pi * order * (x.astype(F32) + 0.5) / NX)
    lane_z = lanes((128, 128))
    mode = lax.broadcasted_iota(jnp.int32, (128, 128), 0)
    order = ((mode % 64) // 8).astype(F32)
    table = jnp.cos(jnp.pi * order * ((lane_z % 64).astype(F32) + 0.5) / LZ)
    table = jnp.where(mode // 64 == lane_z // 64, table, 0.0)
    lane = lanes((ROWS, 128))
    y = start_y + lax.broadcasted_iota(jnp.int32, (ROWS, 128), 0) + (lane // 64) * HALF
    inside_y = one((y >= 0) & (y < NY))
    for first in range(0, EXT, EXT // 2):
        for i in range(EXT // 2):
            work_ref[i * ROWS : (i + 1) * ROWS] = base * xrow_ref[first + i : first + i + 1, :]
        log = jnp.dot(work_ref[...], table, **exact)
        for i in range(EXT // 2):
            xg = start_x + first + i
            live = inside_y * one((xg >= 0) & (xg < NX))
            value = jnp.exp(log[i * ROWS : (i + 1) * ROWS])
            out_ref[first + i] = jnp.where(live > 0.0, 0.5 * value, 0.0)


def rel(h):
    return jnp.exp(jnp.minimum(h, 0.0))


def one(condition):
    return condition.astype(F32)


def split(ref, at, value):
    big = value.astype(jnp.bfloat16)
    ref[at, 0:128] = big
    ref[at, 128:256] = (value - big.astype(F32)).astype(jnp.bfloat16)


def edges():
    z = lanes((8, 128)) % 64
    return one(z < LZ - 1), one(z > 0)


def grid_tables(count_ref, mask_ref):
    north = lax.axis_index("north")
    lane = lanes((ROWS, 128))
    y = north * CY - 8 + lax.broadcasted_iota(jnp.int32, (ROWS, 128), 0) + (lane // 64) * HALF
    z = lane % 64
    count_ref[...] = one(y > 0) + one(y < NY - 1) + one(z > 0) + one(z < LZ - 1)
    mask_ref[...] = one((y >= 0) & (y < NY))


def clear_pads(refs):
    zero = jnp.zeros((8, 128), F32)
    for ref in refs:
        for i in range(ref.shape[0]):
            ref[i, 0:8] = zero
            ref[i, PAD - 8 : PAD] = zero


def start_row(at, h, s, nlo, nhi, cond, ha, ka, sto_ref, src_ref):
    low = lanes((8, 128)) < 64
    north = lax.axis_index("north")
    nlo = jnp.where(north > 0, nlo, 0.0)
    nhi = jnp.where(north < 15, nhi, 0.0)
    pieces = [(0, jnp.where(low, nlo, swap(h[HALF - 8 :])))]
    pieces += [(8 + r, h[r : r + 8]) for r in range(0, HALF, 8)]
    pieces += [(ROWS - 8, swap(jnp.where(low, nhi, h[:8])))]
    if s is not None:
        sources = [swap(jnp.where(low, s[HALF - 8 :], nlo))]
        sources += [s[r : r + 8] for r in range(0, HALF, 8)]
        sources += [jnp.where(low, swap(s[:8]), nhi)]
    for n, (r, piece) in enumerate(pieces):
        relative = rel(piece)
        ha[at, 4 + r : 12 + r] = piece
        ka[at, 4 + r : 12 + r] = cond(r) * relative
        if s is not None:
            sto = 0.5 + 0.5 * relative
            sto_ref[at, r : r + 8] = sto
            src_ref[at, r : r + 8] = sto * piece + sources[n]


def sweep_row(at, xi, hin, kin, hout, kout, cond_ref, sto_ref, src_ref, count_ref, mask_ref):
    up_mask, down_mask = edges()
    gravity = up_mask - down_mask
    xg = lax.axis_index("east") * CX - WIDE + xi
    along_x = one(xg > 0) + one(xg < NX - 1)
    in_x = one((xg >= 0) & (xg < NX))
    for a in range(8, PAD - 8, 8):
        r = a - 4
        h, k = hin[at, a : a + 8], kin[at, a : a + 8]
        hu = pltpu.roll(h, 127, 1) * up_mask
        ku = pltpu.roll(k, 127, 1) * up_mask
        hd = pltpu.roll(h, 1, 1) * down_mask
        kd = pltpu.roll(k, 1, 1) * down_mask
        hn, kn = hin[at, a + 1 : a + 9], kin[at, a + 1 : a + 9]
        hs, ks = hin[at, a - 1 : a + 7], kin[at, a - 1 : a + 7]
        he, ke = hin[at + 1, a : a + 8], kin[at + 1, a : a + 8]
        hw, kw = hin[at - 1, a : a + 8], kin[at - 1, a : a + 8]
        sum_h = ((hu + hd) + (hn + hs)) + ((he + hw) + gravity)
        sum_k = ((ku + kd) + (kn + ks)) + (ke + kw)
        flux = ((ku * hu + kd * hd) + (kn * hn + ks * hs)) + (ke * he + kw * hw)
        top = (src_ref[at, r : r + 8] + k * sum_h) + (flux + (ku - kd))
        below = (count_ref[r : r + 8] + along_x) * k + (sto_ref[at, r : r + 8] + sum_k)
        inv = pltpu.reciprocal(below, approx=True)
        inv = inv * (2.0 - below * inv)
        inv = inv * (2.0 - below * inv)
        new = top * inv * in_x
        if a == 8 or a == PAD - 16:
            new = new * mask_ref[r : r + 8]
        hout[at, a : a + 8] = new
        kout[at, a : a + 8] = cond_ref[xi, r : r + 8] * rel(new)


def velocity_row(at, row, size, h_ref, k_ref, table_ref):
    up_mask, down_mask = edges()
    up_mask = jnp.concatenate([up_mask, up_mask], axis=0)
    down_mask = jnp.concatenate([down_mask, down_mask], axis=0)
    for r in range(0, HALF, 16):
        a = r + 12
        h, k = h_ref[at, a : a + 16], k_ref[at, a : a + 16]
        hu = pltpu.roll(h, 127, 1) * up_mask
        hd = pltpu.roll(h, 1, 1) * down_mask
        flow_x = -k * (h_ref[at + 1, a : a + 16] - h_ref[at - 1, a : a + 16])
        flow_y = -k * (h_ref[at, a + 1 : a + 17] - h_ref[at, a - 1 : a + 15])
        flow_z = -k * ((hu - hd) + 2.0)
        for c, flow in enumerate((flow_x, flow_y, flow_z)):
            split(table_ref, pl.ds(pl.multiple_of(row + c * size + r, 16), 16), flow)


def inner_kernel(
    ht_ref, st_ref, nlo_ref, nhi_ref, cond_ref,
    ha, hb, ka, kb, sto_ref, src_ref, table_ref,
    count_ref, mask_ref,
):
    grid_tables(count_ref, mask_ref)
    clear_pads((hb, kb))

    def own(x, carry):
        cond = lambda r: cond_ref[x + WIDE, r : r + 8]
        start_row(x, ht_ref[x], st_ref[x], nlo_ref[x], nhi_ref[x], cond, ha, ka, sto_ref, src_ref)
        return carry

    lax.fori_loop(0, CX, own, 0)
    hin, kin, hout, kout = ha, ka, hb, kb
    for number in range(1, ITERS + 1):

        def sweep(x, carry, hin=hin, kin=kin, hout=hout, kout=kout):
            sweep_row(x, x + WIDE, hin, kin, hout, kout, cond_ref, sto_ref, src_ref, count_ref, mask_ref)
            return carry

        lax.fori_loop(number, CX - number, sweep, 0)
        hin, kin, hout, kout = hout, kout, hin, kin

    def velocity(i, carry):
        velocity_row(i + WIDE, i * HALF, MID * HALF, hin, kin, table_ref)
        return carry

    lax.fori_loop(0, MID, velocity, 0)


def outer_kernel(
    ha0, hb0, ka0, kb0, sto0, src0, elo_ref, ehi_ref, cond_ref,
    heads_ref, table_ref,
    ha, hb, ka, kb, sto_ref, src_ref, count_ref, mask_ref,
):
    east = lax.axis_index("east")
    grid_tables(count_ref, mask_ref)
    clear_pads((hb, kb))
    for x in range(CX):
        depth = min(x, CX - 1 - x)
        if depth <= WIDE:
            ha[x + WIDE], ka[x + WIDE] = ha0[x], ka0[x]
        if 1 <= depth <= ITERS:
            hb[x + WIDE], kb[x + WIDE] = hb0[x], kb0[x]
    for small, big in ((sto0, sto_ref), (src0, src_ref)):
        for i in range(ITERS):
            big[WIDE + i] = small[i]
            big[EXT - 1 - WIDE - i] = small[CX - 1 - i]
    zero = jnp.zeros((8, 128), F32)
    for ref, valid, first, flip in ((elo_ref, east > 0, 0, 0), (ehi_ref, east < 15, EXT - WIDE, 1)):
        for i in range(WIDE):
            xi = first + i
            h = jnp.where(valid, ref[i * HALF : (i + 1) * HALF], 0.0)
            s, corner = None, zero
            j = i if flip else i - 1
            if 0 <= j < NSIDE:
                s_at = (WIDE + j) * HALF
                c_at = (WIDE + NSIDE) * HALF + j * 8
                s = jnp.where(valid, ref[s_at : s_at + HALF], 0.0)
                corner = jnp.where(valid, ref[c_at : c_at + 8], 0.0)
            cond = lambda r, xi=xi: cond_ref[xi, r : r + 8]
            start_row(xi, h, s, corner, corner, cond, ha, ka, sto_ref, src_ref)

    hin, kin, hout, kout = ha, ka, hb, kb
    for number in range(1, ITERS + 1):

        def sweep(i, carry, number=number, hin=hin, kin=kin, hout=hout, kout=kout):
            xi = number + i + jnp.where(i < WIDE, 0, EXT - 2 * WIDE - 2 * number)
            sweep_row(xi, xi, hin, kin, hout, kout, cond_ref, sto_ref, src_ref, count_ref, mask_ref)
            return carry

        lax.fori_loop(0, 2 * WIDE, sweep, 0)
        hin, kin, hout, kout = hout, kout, hin, kin

    for x in range(CX):
        source, at = (ha0, x) if WIDE <= x < CX - WIDE else (hin, x + WIDE)
        heads_ref[x] = source[at, 12 : 12 + HALF]

    def velocity(i, carry):
        at = i + WIDE + jnp.where(i < WIDE, 0, MID)
        velocity_row(at, i * HALF, OUT * HALF, hin, kin, table_ref)
        return carry

    lax.fori_loop(0, OUT, velocity, 0)


def onehot_pair(index):
    hot = lax.broadcasted_iota(jnp.int32, (128, index.shape[1]), 0) == index
    hot = jnp.where(hot, 1.0, 0.0).astype(jnp.bfloat16)
    return jnp.concatenate([hot, hot], axis=0)


def choose(get, first, count, bits):
    if count == 1:
        return get(first)
    level = (count - 1).bit_length() - 1
    half = 1 << level
    low = choose(get, first, half, bits)
    high = choose(get, first + half, count - half, bits)
    return jnp.where(bits[level], high, low)


BLOCK = 512
PARTS = BLOCK // 128


def read_cells(cell_ref, n):
    cell = jnp.concatenate([cell_ref[pl.ds(n * PARTS + i, 1), :] for i in range(PARTS)], axis=1)
    layer, x, j = cell >> 11, (cell >> 7) & 15, cell & 127
    return x, j & 63, (j >> 6) * 64 + layer


def sampled_at(table_ref, count, place, inner_y, lane):
    got = jnp.dot(table_ref[...], onehot_pair(lane), preferred_element_type=F32)
    row8 = jnp.broadcast_to(place * 64 + inner_y, (8, BLOCK))
    bits = [(row8 & (8 << b)) != 0 for b in range(7)]
    mine = lax.broadcasted_iota(jnp.int32, (8, BLOCK), 0) == (row8 & 7)
    size = count * HALF
    for c in range(3):
        picked = choose(lambda g: got[c * size + g * 8 : c * size + g * 8 + 8], 0, count * 8, bits)
        yield c, jnp.sum(jnp.where(mine, picked, 0.0), axis=0, keepdims=True)


def sample_inner_kernel(table_ref, cell_ref, part_ref):
    def block(n, carry):
        x, inner_y, lane = read_cells(cell_ref, n)
        at = pl.ds(pl.multiple_of(n * BLOCK, BLOCK), BLOCK)
        for c, sampled in sampled_at(table_ref, MID, jnp.clip(x - WIDE, 0, MID - 1), inner_y, lane):
            part_ref[c : c + 1, at] = sampled
        return carry

    lax.fori_loop(0, 4096 // BLOCK, block, 0, unroll=2)


def sample_kernel(
    table_ref, cell_ref, part_ref, rec_ref, couple_ref, list_ref, count_ref, moved_ref, send_ref, pick_ref
):
    def block(n, carry):
        x, inner_y, lane = read_cells(cell_ref, n)
        middle = (x >= WIDE) & (x < CX - WIDE)
        place = jnp.where(x < WIDE, x, jnp.maximum(x - MID, 0))
        at = pl.ds(pl.multiple_of(n * BLOCK, BLOCK), BLOCK)
        total = rec_ref[:, at]
        for c, outer in sampled_at(table_ref, OUT, place, inner_y, lane):
            sampled = jnp.where(middle, part_ref[c : c + 1, at], outer)
            weight = couple_ref[c * 32 : (c + 1) * 32, :]
            total = total + jnp.concatenate([weight] * PARTS, axis=1) * sampled
        moved_ref[:, at] = total
        for i in range(PARTS):
            rows = pl.ds(pl.multiple_of((n * PARTS + i) * 32, 32), 32)
            split(pick_ref, rows, total[:, i * 128 : (i + 1) * 128])
        return carry

    lax.fori_loop(0, 4096 // BLOCK, block, 0, unroll=2)
    for d in range(4):
        index = list_ref[d : d + 1, :]
        got = jnp.dot(pick_ref[...], onehot_pair(index & 127), preferred_element_type=F32)
        block_of = jnp.broadcast_to(index >> 7, (32, BLOCK))
        bits = [(block_of & (1 << b)) != 0 for b in range(5)]
        picked = choose(lambda g: got[g * 32 : (g + 1) * 32], 0, 32, bits)
        live = lanes((32, BLOCK)) < count_ref[d, 0]
        send_ref[d] = jnp.where(live, picked, 0.0)


def back_kernel(ht_ref, out_ref):
    for x in range(CX):
        t = ht_ref[x].T
        out_ref[pl.ds(x, LZ, stride=CX), :] = jnp.concatenate([t[:LZ], t[LZ:]], axis=1)


def arrive_kernel(a_ref, b_ref, c_ref, d_ref, out_ref):
    east, north = lax.axis_index("east"), lax.axis_index("north")
    for d, (ref, valid) in enumerate(
        ((a_ref, east > 0), (b_ref, east < 15), (c_ref, north > 0), (d_ref, north < 15))
    ):
        out_ref[d] = jnp.where(valid, ref[...], 0.0)


def call(kernel, outs, ins, scratch=(), limit=6, specs=None):
    return pl.pallas_call(
        kernel,
        out_shape=[jax.ShapeDtypeStruct(s, t) for s, t in outs],
        in_specs=specs or [VMEM] * len(ins),
        out_specs=[VMEM] * len(outs),
        scratch_shapes=list(scratch),
        compiler_params=pltpu.CompilerParams(vmem_limit_bytes=limit * 2**20),
    )(*ins)


def ring(value, axis, steps):
    count = lax.axis_size(axis)
    return lax.ppermute(value, axis, [(i, (i + steps) % count) for i in range(count)])


def on_device(head_old, source, mode_coeffs, records, cell_index, coupling, send_list, send_count):
    flat = (LZ * CX, CY)
    tile = ((CX, HALF, 128), F32)
    side = ((CX, 8, 128), F32)
    (ht,) = call(turn_kernel, [tile], [head_old.reshape(flat)])
    st, n_up, n_down = call(turn_source_kernel, [tile, side, side], [source.reshape(flat), ht])
    nlo = ring(n_up, "north", 1)
    nhi = ring(n_down, "north", -1)
    (cond,) = call(
        cond_kernel,
        [((EXT, ROWS, 128), F32)],
        [mode_coeffs.reshape(64, 8)],
        [pltpu.VMEM((EXT // 2 * ROWS, 128), F32), pltpu.VMEM((32, 128), F32)],
        limit=12,
    )
    nlo, nhi, cond = lax.optimization_barrier((nlo, nhi, cond))
    edge = ((ESEND, 128), F32)
    e_up, e_down = call(pack_kernel, [edge, edge], [ht, st, nlo, nhi])
    elo = ring(e_up, "east", 1)
    ehi = ring(e_down, "east", -1)
    plane = pltpu.VMEM((ROWS, 128), F32)
    level = ((CX, PAD, 128), F32)
    base = ((CX, ROWS, 128), F32)
    cells = cell_index.reshape(32, 128)
    *inner, table_mid = call(
        inner_kernel,
        [level] * 4 + [base] * 2 + [((3 * MID * HALF, 256), jnp.bfloat16)],
        [ht, st, nlo, nhi, cond],
        [plane, plane],
        limit=12,
    )
    (part,) = call(sample_inner_kernel, [((8, 4096), F32)], [table_mid, cells], limit=20)
    buf = pltpu.VMEM((EXT, PAD, 128), F32)
    ext = pltpu.VMEM((EXT, ROWS, 128), F32)
    heads, table = call(
        outer_kernel,
        [tile, ((3 * OUT * HALF, 256), jnp.bfloat16)],
        list(inner) + [elo, ehi, cond],
        [buf, buf, buf, buf, ext, ext, plane, plane],
        limit=20,
    )
    couple = jnp.broadcast_to((STEP * coupling)[:, :, None], (3, 32, 128)).reshape(96, 128)
    moved, buffers = call(
        sample_kernel,
        [((32, 4096), F32), ((4, 32, 512), F32)],
        [table, cells, part, records, couple, send_list, send_count],
        [pltpu.VMEM((1024, 256), jnp.bfloat16)],
        limit=32,
        specs=[VMEM] * 6 + [SMEM],
    )
    came = [
        ring(buffers[0], "east", 1),
        ring(buffers[1], "east", -1),
        ring(buffers[2], "north", 1),
        ring(buffers[3], "north", -1),
    ]
    (heads_out,) = call(back_kernel, [(flat, F32)], [heads])
    (arrivals,) = call(arrive_kernel, [((4, 32, 512), F32)], came)
    return (heads_out.reshape(LZ, CX, CY), moved, arrivals)


def solution(mesh):
    return jax.shard_map(
        on_device,
        mesh=mesh,
        in_specs=(
            P(None, "east", "north"),
            P(None, "east", "north"),
            P(),
            P(None, ("east", "north")),
            P(("east", "north")),
            P(),
            P(None, ("east", "north")),
            P(None, ("east", "north")),
        ),
        out_specs=(
            P(None, "east", "north"),
            P(None, ("east", "north")),
            P(None, None, ("east", "north")),
        ),
        check_vma=False,
    )
```

```python
import jax
import jax.numpy as jnp
from jax import lax
from jax.experimental import pallas as pl
from jax.experimental.pallas import tpu as pltpu
from jax.sharding import PartitionSpec as P

ITERS = 4
LZ, CX, CY = 64, 16, 128
HALF = CY // 2
WIDE = ITERS + 1
EXT = CX + 2 * WIDE
ROWS = HALF + 16
PAD = ROWS + 8
MID = CX - 2 * WIDE
OUT = CX - MID
NX, NY = 256, 2048
SPAN = HALF + 8
ESEND = 7 * SPAN
STEP = 0.25
F32 = jnp.float32
VMEM = pl.BlockSpec(memory_space=pltpu.VMEM)
SMEM = pl.BlockSpec(memory_space=pltpu.SMEM)


def lanes(shape):
    return lax.broadcasted_iota(jnp.int32, shape, len(shape) - 1)


def swap(v):
    return pltpu.roll(v, 64, 1)


def turned(ref, x):
    t = ref[pl.ds(x, LZ, stride=CX), :].T
    return jnp.concatenate([t[:HALF], t[HALF:]], axis=1)


def turn_kernel(h_ref, ht_ref):
    for x in range(CX):
        ht_ref[x] = turned(h_ref, x)


def turn_source_kernel(s_ref, ht_ref, st_ref, nlo_ref, nhi_ref):
    low = lanes((8, 128)) < 64
    for x in range(CX):
        s = turned(s_ref, x)
        st_ref[x] = s
        nlo_ref[x] = jnp.where(low, swap(ht_ref[x, HALF - 8 :]), s[HALF - 8 :])
        nhi_ref[x] = jnp.where(low, ht_ref[x, :8], swap(s[:8]))


def cond_kernel(modes_ref, out_ref, work_ref, xrow_ref):
    start_x = lax.axis_index("east") * CX - WIDE
    start_y = lax.axis_index("north") * CY - 8
    exact = dict(precision=lax.Precision.HIGHEST, preferred_element_type=F32)
    ca = lax.broadcasted_iota(jnp.int32, (64, 8), 0)
    order_c, order_a, order_b = (ca // 8).astype(F32), (ca % 8).astype(F32), lanes((64, 8)).astype(F32)
    spectrum = 1.0 / (1.0 + (order_c * order_c + order_a * order_a + order_b * order_b) / 4.0)
    total = jnp.sum(jnp.sum(spectrum, axis=1, keepdims=True), axis=0, keepdims=True)
    weights = modes_ref[...] * jnp.sqrt(spectrum) * (1.0 / jnp.sqrt(total))
    row = lax.broadcasted_iota(jnp.int32, (ROWS, 8), 0)
    order = lanes((ROWS, 8)).astype(F32)
    halves = []
    for half in range(2):
        coord = (start_y + half * HALF + row).astype(F32) + 0.5
        table = jnp.cos(jnp.pi * order * coord / NY)
        halves.append(lax.dot_general(table, weights, (((1,), (1,)), ((), ())), **exact))
    base = jnp.concatenate(halves, axis=1)
    x = start_x + lax.broadcasted_iota(jnp.int32, (32, 128), 0)
    order = (lanes((32, 128)) % 8).astype(F32)
    xrow_ref[...] = jnp.cos(jnp.pi * order * (x.astype(F32) + 0.5) / NX)
    lane_z = lanes((128, 128))
    mode = lax.broadcasted_iota(jnp.int32, (128, 128), 0)
    order = ((mode % 64) // 8).astype(F32)
    table = jnp.cos(jnp.pi * order * ((lane_z % 64).astype(F32) + 0.5) / LZ)
    table = jnp.where(mode // 64 == lane_z // 64, table, 0.0)
    lane = lanes((ROWS, 128))
    y = start_y + lax.broadcasted_iota(jnp.int32, (ROWS, 128), 0) + (lane // 64) * HALF
    inside_y = one((y >= 0) & (y < NY))
    for first in range(0, EXT, EXT // 2):
        for i in range(EXT // 2):
            work_ref[i * ROWS : (i + 1) * ROWS] = base * xrow_ref[first + i : first + i + 1, :]
        log = jnp.dot(work_ref[...], table, **exact)
        for i in range(EXT // 2):
            xg = start_x + first + i
            live = inside_y * one((xg >= 0) & (xg < NX))
            value = jnp.exp(log[i * ROWS : (i + 1) * ROWS])
            out_ref[first + i] = jnp.where(live > 0.0, 0.5 * value, 0.0)


def rel(h):
    return jnp.exp(jnp.minimum(h, 0.0))


def one(condition):
    return condition.astype(F32)


def split(ref, at, value):
    big = value.astype(jnp.bfloat16)
    ref[at, 0:128] = big
    ref[at, 128:256] = (value - big.astype(F32)).astype(jnp.bfloat16)


def edges():
    z = lanes((8, 128)) % 64
    return one(z < LZ - 1), one(z > 0)


def grid_tables(count_ref, mask_ref):
    north = lax.axis_index("north")
    lane = lanes((ROWS, 128))
    y = north * CY - 8 + lax.broadcasted_iota(jnp.int32, (ROWS, 128), 0) + (lane // 64) * HALF
    z = lane % 64
    count_ref[...] = one(y > 0) + one(y < NY - 1) + one(z > 0) + one(z < LZ - 1)
    mask_ref[...] = one((y >= 0) & (y < NY))


def clear_pads(refs):
    zero = jnp.zeros((8, 128), F32)
    for ref in refs:
        for i in range(ref.shape[0]):
            ref[i, 0:8] = zero
            ref[i, PAD - 8 : PAD] = zero


def start_row(at, h, s, nlo, nhi, cond, ha, ka, sto_ref, src_ref):
    low = lanes((8, 128)) < 64
    north = lax.axis_index("north")
    nlo = jnp.where(north > 0, nlo, 0.0)
    nhi = jnp.where(north < 15, nhi, 0.0)
    pieces = [(0, jnp.where(low, nlo, swap(h[HALF - 8 :])))]
    pieces += [(8 + r, h[r : r + 8]) for r in range(0, HALF, 8)]
    pieces += [(ROWS - 8, swap(jnp.where(low, nhi, h[:8])))]
    if s is not None:
        sources = [swap(jnp.where(low, s[HALF - 8 :], nlo))]
        sources += [s[r : r + 8] for r in range(0, HALF, 8)]
        sources += [jnp.where(low, swap(s[:8]), nhi)]
    for n, (r, piece) in enumerate(pieces):
        relative = rel(piece)
        ha[at, 4 + r : 12 + r] = piece
        ka[at, 4 + r : 12 + r] = cond(r) * relative
        if s is not None:
            sto = 0.5 + 0.5 * relative
            sto_ref[at, r : r + 8] = sto
            src_ref[at, r : r + 8] = sto * piece + sources[n]


def sweep_row(at, xi, hin, kin, hout, kout, cond_ref, sto_ref, src_ref, count_ref, mask_ref):
    up_mask, down_mask = edges()
    gravity = up_mask - down_mask
    xg = lax.axis_index("east") * CX - WIDE + xi
    along_x = one(xg > 0) + one(xg < NX - 1)
    in_x = one((xg >= 0) & (xg < NX))
    for a in range(8, PAD - 8, 8):
        r = a - 4
        h, k = hin[at, a : a + 8], kin[at, a : a + 8]
        hu = pltpu.roll(h, 127, 1) * up_mask
        ku = pltpu.roll(k, 127, 1) * up_mask
        hd = pltpu.roll(h, 1, 1) * down_mask
        kd = pltpu.roll(k, 1, 1) * down_mask
        hn, kn = hin[at, a + 1 : a + 9], kin[at, a + 1 : a + 9]
        hs, ks = hin[at, a - 1 : a + 7], kin[at, a - 1 : a + 7]
        he, ke = hin[at + 1, a : a + 8], kin[at + 1, a : a + 8]
        hw, kw = hin[at - 1, a : a + 8], kin[at - 1, a : a + 8]
        sum_h = ((hu + hd) + (hn + hs)) + ((he + hw) + gravity)
        sum_k = ((ku + kd) + (kn + ks)) + (ke + kw)
        flux = ((ku * hu + kd * hd) + (kn * hn + ks * hs)) + (ke * he + kw * hw)
        top = (src_ref[at, r : r + 8] + k * sum_h) + (flux + (ku - kd))
        below = (count_ref[r : r + 8] + along_x) * k + (sto_ref[at, r : r + 8] + sum_k)
        inv = pltpu.reciprocal(below, approx=True)
        inv = inv * (2.0 - below * inv)
        inv = inv * (2.0 - below * inv)
        new = top * inv * in_x
        if a == 8 or a == PAD - 16:
            new = new * mask_ref[r : r + 8]
        hout[at, a : a + 8] = new
        kout[at, a : a + 8] = cond_ref[xi, r : r + 8] * rel(new)


def velocity_row(at, row, size, h_ref, k_ref, table_ref):
    up_mask, down_mask = edges()
    up_mask = jnp.concatenate([up_mask, up_mask], axis=0)
    down_mask = jnp.concatenate([down_mask, down_mask], axis=0)
    for r in range(0, HALF, 16):
        a = r + 12
        h, k = h_ref[at, a : a + 16], k_ref[at, a : a + 16]
        hu = pltpu.roll(h, 127, 1) * up_mask
        hd = pltpu.roll(h, 1, 1) * down_mask
        flow_x = -k * (h_ref[at + 1, a : a + 16] - h_ref[at - 1, a : a + 16])
        flow_y = -k * (h_ref[at, a + 1 : a + 17] - h_ref[at, a - 1 : a + 15])
        flow_z = -k * ((hu - hd) + 2.0)
        for c, flow in enumerate((flow_x, flow_y, flow_z)):
            split(table_ref, pl.ds(pl.multiple_of(row + c * size + r, 16), 16), flow)


def own_row(x, at, ht_ref, st_ref, nlo_ref, nhi_ref, cond_ref, ha, ka, sto_ref, src_ref):
    cond = lambda r: cond_ref[x + WIDE, r : r + 8]
    start_row(at, ht_ref[x], st_ref[x], nlo_ref[x], nhi_ref[x], cond, ha, ka, sto_ref, src_ref)


def edge_kernel(
    ht_ref, st_ref, nlo_ref, nhi_ref, cond_ref, up_ref, down_ref,
    ha, hb, ka, kb, sto_ref, src_ref, count_ref, mask_ref,
):
    grid_tables(count_ref, mask_ref)
    clear_pads((hb, kb))
    tables = (cond_ref, sto_ref, src_ref, count_ref, mask_ref)
    for send_ref, first_x, a, b in ((up_ref, CX - WIDE, WIDE - 1, WIDE - 2), (down_ref, 0, 0, 1)):

        def own(at, carry, first_x=first_x):
            own_row(first_x + at, at, ht_ref, st_ref, nlo_ref, nhi_ref, cond_ref, ha, ka, sto_ref, src_ref)
            return carry

        lax.fori_loop(0, WIDE, own, 0)

        def sweep(at, carry, first_x=first_x):
            sweep_row(at, WIDE + first_x + at, ha, ka, hb, kb, *tables)
            return carry

        lax.fori_loop(1, 4, sweep, 0)
        sweep_row(2, WIDE + first_x + 2, hb, kb, ha, ka, *tables)
        parts = ((ha, a, 8), (ha, b, 8), (src_ref, a, 4), (src_ref, b, 4), (hb, b, 8), (hb, 2, 8), (ha, 2, 8))
        for n, (source, at, r) in enumerate(parts):
            send_ref[n * SPAN : (n + 1) * SPAN] = source[at, r : r + SPAN]


def inner_kernel(
    ht_ref, st_ref, nlo_ref, nhi_ref, cond_ref,
    ha, hb, ka, kb, sto_ref, src_ref, table_ref,
    count_ref, mask_ref,
):
    grid_tables(count_ref, mask_ref)
    clear_pads((hb, kb))

    def own(x, carry):
        cond = lambda r: cond_ref[x + WIDE, r : r + 8]
        start_row(x, ht_ref[x], st_ref[x], nlo_ref[x], nhi_ref[x], cond, ha, ka, sto_ref, src_ref)
        return carry

    lax.fori_loop(0, CX, own, 0)
    hin, kin, hout, kout = ha, ka, hb, kb
    for number in range(1, ITERS + 1):

        def sweep(x, carry, hin=hin, kin=kin, hout=hout, kout=kout):
            sweep_row(x, x + WIDE, hin, kin, hout, kout, cond_ref, sto_ref, src_ref, count_ref, mask_ref)
            return carry

        lax.fori_loop(number, CX - number, sweep, 0)
        hin, kin, hout, kout = hout, kout, hin, kin

    def velocity(i, carry):
        velocity_row(i + WIDE, i * HALF, MID * HALF, hin, kin, table_ref)
        return carry

    lax.fori_loop(0, MID, velocity, 0)


def outer_kernel(
    ha0, hb0, ka0, kb0, sto0, src0, elo_ref, ehi_ref, cond_ref,
    heads_ref, table_ref,
    ha, hb, ka, kb, sto_ref, src_ref, count_ref, mask_ref,
):
    east = lax.axis_index("east")
    grid_tables(count_ref, mask_ref)
    clear_pads((ha, hb, ka, kb))
    for x in range(CX):
        depth = min(x, CX - 1 - x)
        if depth <= WIDE:
            ha[x + WIDE], ka[x + WIDE] = ha0[x], ka0[x]
        if 1 <= depth <= ITERS:
            hb[x + WIDE], kb[x + WIDE] = hb0[x], kb0[x]
    for small, big in ((sto0, sto_ref), (src0, src_ref)):
        for i in range(ITERS):
            big[WIDE + i] = small[i]
            big[EXT - 1 - WIDE - i] = small[CX - 1 - i]
    for ref, valid, near, out in ((elo_ref, east > 0, WIDE - 1, -1), (ehi_ref, east < 15, EXT - WIDE, 1)):
        block = lambda n, ref=ref, valid=valid: jnp.where(valid, ref[n * SPAN : (n + 1) * SPAN], 0.0)
        for n, big_h, big_k, depth in ((0, ha, ka, 0), (1, ha, ka, 1), (4, hb, kb, 1), (5, hb, kb, 2), (6, ha, ka, 2)):
            xi = near + out * depth
            h = block(n)
            relative = rel(h)
            big_h[xi, 8 : 8 + SPAN] = h
            big_k[xi, 8 : 8 + SPAN] = cond_ref[xi, 4 : 4 + SPAN] * relative
            if n < 2:
                sto_ref[xi, 4 : 4 + SPAN] = 0.5 + 0.5 * relative
                src_ref[xi, 4 : 4 + SPAN] = block(n + 2)

    hin, kin, hout, kout = ha, ka, hb, kb
    for first, count in ((4, 2), (3, 4), (3, 5), (4, 5)):

        def sweep(i, carry, first=first, count=count, hin=hin, kin=kin, hout=hout, kout=kout):
            xi = jnp.where(i < count, first + i, EXT - 1 - first - (i - count))
            sweep_row(xi, xi, hin, kin, hout, kout, cond_ref, sto_ref, src_ref, count_ref, mask_ref)
            return carry

        lax.fori_loop(0, 2 * count, sweep, 0)
        hin, kin, hout, kout = hout, kout, hin, kin

    for x in range(CX):
        source, at = (ha0, x) if WIDE <= x < CX - WIDE else (hin, x + WIDE)
        heads_ref[x] = source[at, 12 : 12 + HALF]

    def velocity(i, carry):
        at = i + WIDE + jnp.where(i < WIDE, 0, MID)
        velocity_row(at, i * HALF, OUT * HALF, hin, kin, table_ref)
        return carry

    lax.fori_loop(0, OUT, velocity, 0)


def onehot_pair(index):
    hot = lax.broadcasted_iota(jnp.int32, (128, index.shape[1]), 0) == index
    hot = jnp.where(hot, 1.0, 0.0).astype(jnp.bfloat16)
    return jnp.concatenate([hot, hot], axis=0)


def choose(get, first, count, bits):
    if count == 1:
        return get(first)
    level = (count - 1).bit_length() - 1
    half = 1 << level
    low = choose(get, first, half, bits)
    high = choose(get, first + half, count - half, bits)
    return jnp.where(bits[level], high, low)


BLOCK = 512
PARTS = BLOCK // 128


def read_cells(cell_ref, n):
    cell = jnp.concatenate([cell_ref[pl.ds(n * PARTS + i, 1), :] for i in range(PARTS)], axis=1)
    layer, x, j = cell >> 11, (cell >> 7) & 15, cell & 127
    return x, j & 63, (j >> 6) * 64 + layer


def sampled_at(table_ref, count, place, inner_y, lane):
    got = jnp.dot(table_ref[...], onehot_pair(lane), preferred_element_type=F32)
    row8 = jnp.broadcast_to(place * 64 + inner_y, (8, BLOCK))
    bits = [(row8 & (8 << b)) != 0 for b in range(7)]
    mine = lax.broadcasted_iota(jnp.int32, (8, BLOCK), 0) == (row8 & 7)
    size = count * HALF
    for c in range(3):
        picked = choose(lambda g: got[c * size + g * 8 : c * size + g * 8 + 8], 0, count * 8, bits)
        yield c, jnp.sum(jnp.where(mine, picked, 0.0), axis=0, keepdims=True)


def sample_inner_kernel(table_ref, cell_ref, part_ref):
    def block(n, carry):
        x, inner_y, lane = read_cells(cell_ref, n)
        at = pl.ds(pl.multiple_of(n * BLOCK, BLOCK), BLOCK)
        for c, sampled in sampled_at(table_ref, MID, jnp.clip(x - WIDE, 0, MID - 1), inner_y, lane):
            part_ref[c : c + 1, at] = sampled
        return carry

    lax.fori_loop(0, 4096 // BLOCK, block, 0, unroll=2)


def sample_kernel(
    table_ref, cell_ref, part_ref, rec_ref, couple_ref, list_ref, count_ref, moved_ref, send_ref, pick_ref
):
    def block(n, carry):
        x, inner_y, lane = read_cells(cell_ref, n)
        middle = (x >= WIDE) & (x < CX - WIDE)
        place = jnp.where(x < WIDE, x, jnp.maximum(x - MID, 0))
        at = pl.ds(pl.multiple_of(n * BLOCK, BLOCK), BLOCK)
        total = rec_ref[:, at]
        for c, outer in sampled_at(table_ref, OUT, place, inner_y, lane):
            sampled = jnp.where(middle, part_ref[c : c + 1, at], outer)
            weight = couple_ref[c * 32 : (c + 1) * 32, :]
            total = total + jnp.concatenate([weight] * PARTS, axis=1) * sampled
        moved_ref[:, at] = total
        for i in range(PARTS):
            rows = pl.ds(pl.multiple_of((n * PARTS + i) * 32, 32), 32)
            split(pick_ref, rows, total[:, i * 128 : (i + 1) * 128])
        return carry

    lax.fori_loop(0, 4096 // BLOCK, block, 0, unroll=2)
    for d in range(4):
        index = list_ref[d : d + 1, :]
        got = jnp.dot(pick_ref[...], onehot_pair(index & 127), preferred_element_type=F32)
        block_of = jnp.broadcast_to(index >> 7, (32, BLOCK))
        bits = [(block_of & (1 << b)) != 0 for b in range(5)]
        picked = choose(lambda g: got[g * 32 : (g + 1) * 32], 0, 32, bits)
        live = lanes((32, BLOCK)) < count_ref[d, 0]
        send_ref[d] = jnp.where(live, picked, 0.0)


def back_kernel(ht_ref, out_ref):
    for x in range(CX):
        t = ht_ref[x].T
        out_ref[pl.ds(x, LZ, stride=CX), :] = jnp.concatenate([t[:LZ], t[LZ:]], axis=1)


def arrive_kernel(a_ref, b_ref, c_ref, d_ref, out_ref):
    east, north = lax.axis_index("east"), lax.axis_index("north")
    for d, (ref, valid) in enumerate(
        ((a_ref, east > 0), (b_ref, east < 15), (c_ref, north > 0), (d_ref, north < 15))
    ):
        out_ref[d] = jnp.where(valid, ref[...], 0.0)


def call(kernel, outs, ins, scratch=(), limit=6, specs=None):
    return pl.pallas_call(
        kernel,
        out_shape=[jax.ShapeDtypeStruct(s, t) for s, t in outs],
        in_specs=specs or [VMEM] * len(ins),
        out_specs=[VMEM] * len(outs),
        scratch_shapes=list(scratch),
        compiler_params=pltpu.CompilerParams(vmem_limit_bytes=limit * 2**20),
    )(*ins)


def ring(value, axis, steps):
    count = lax.axis_size(axis)
    return lax.ppermute(value, axis, [(i, (i + steps) % count) for i in range(count)])


def on_device(head_old, source, mode_coeffs, records, cell_index, coupling, send_list, send_count):
    flat = (LZ * CX, CY)
    tile = ((CX, HALF, 128), F32)
    side = ((CX, 8, 128), F32)
    (ht,) = call(turn_kernel, [tile], [head_old.reshape(flat)])
    st, n_up, n_down = call(turn_source_kernel, [tile, side, side], [source.reshape(flat), ht])
    nlo = ring(n_up, "north", 1)
    nhi = ring(n_down, "north", -1)
    (cond,) = call(
        cond_kernel,
        [((EXT, ROWS, 128), F32)],
        [mode_coeffs.reshape(64, 8)],
        [pltpu.VMEM((EXT // 2 * ROWS, 128), F32), pltpu.VMEM((32, 128), F32)],
        limit=12,
    )
    nlo, nhi, cond = lax.optimization_barrier((nlo, nhi, cond))
    edge = ((ESEND, 128), F32)
    plane = pltpu.VMEM((ROWS, 128), F32)
    some, some_base = pltpu.VMEM((WIDE, PAD, 128), F32), pltpu.VMEM((WIDE, ROWS, 128), F32)
    e_up, e_down = call(
        edge_kernel,
        [edge, edge],
        [ht, st, nlo, nhi, cond],
        [some] * 4 + [some_base] * 2 + [plane, plane],
        limit=8,
    )
    elo = ring(e_up, "east", 1)
    ehi = ring(e_down, "east", -1)
    level = ((CX, PAD, 128), F32)
    base = ((CX, ROWS, 128), F32)
    cells = cell_index.reshape(32, 128)
    *inner, table_mid = call(
        inner_kernel,
        [level] * 4 + [base] * 2 + [((3 * MID * HALF, 256), jnp.bfloat16)],
        [ht, st, nlo, nhi, cond],
        [plane, plane],
        limit=12,
    )
    (part,) = call(sample_inner_kernel, [((8, 4096), F32)], [table_mid, cells], limit=20)
    buf = pltpu.VMEM((EXT, PAD, 128), F32)
    ext = pltpu.VMEM((EXT, ROWS, 128), F32)
    heads, table = call(
        outer_kernel,
        [tile, ((3 * OUT * HALF, 256), jnp.bfloat16)],
        list(inner) + [elo, ehi, cond],
        [buf, buf, buf, buf, ext, ext, plane, plane],
        limit=20,
    )
    couple = jnp.broadcast_to((STEP * coupling)[:, :, None], (3, 32, 128)).reshape(96, 128)
    moved, buffers = call(
        sample_kernel,
        [((32, 4096), F32), ((4, 32, 512), F32)],
        [table, cells, part, records, couple, send_list, send_count],
        [pltpu.VMEM((1024, 256), jnp.bfloat16)],
        limit=32,
        specs=[VMEM] * 6 + [SMEM],
    )
    came = [
        ring(buffers[0], "east", 1),
        ring(buffers[1], "east", -1),
        ring(buffers[2], "north", 1),
        ring(buffers[3], "north", -1),
    ]
    (heads_out,) = call(back_kernel, [(flat, F32)], [heads])
    (arrivals,) = call(arrive_kernel, [((4, 32, 512), F32)], came)
    return (heads_out.reshape(LZ, CX, CY), moved, arrivals)


def solution(mesh):
    return jax.shard_map(
        on_device,
        mesh=mesh,
        in_specs=(
            P(None, "east", "north"),
            P(None, "east", "north"),
            P(),
            P(None, ("east", "north")),
            P(("east", "north")),
            P(),
            P(None, ("east", "north")),
            P(None, ("east", "north")),
        ),
        out_specs=(
            P(None, "east", "north"),
            P(None, ("east", "north")),
            P(None, None, ("east", "north")),
        ),
        check_vma=False,
    )
```

```python
import jax
import jax.numpy as jnp
from jax import lax
from jax.experimental import pallas as pl
from jax.experimental.pallas import tpu as pltpu
from jax.sharding import PartitionSpec as P

ITERS = 4
LZ, CX, CY = 64, 16, 128
HALF = CY // 2
WIDE = ITERS + 1
EXT = CX + 2 * WIDE
ROWS = HALF + 16
PAD = ROWS + 8
MID = CX - 2 * WIDE
OUT = CX - MID
NX, NY = 256, 2048
SPAN = HALF + 8
ESEND = 7 * SPAN
STEP = 0.25
F32 = jnp.float32
VMEM = pl.BlockSpec(memory_space=pltpu.VMEM)
SMEM = pl.BlockSpec(memory_space=pltpu.SMEM)


def lanes(shape):
    return lax.broadcasted_iota(jnp.int32, shape, len(shape) - 1)


def swap(v):
    return pltpu.roll(v, 64, 1)


def turned(ref, x):
    t = ref[pl.ds(x, LZ, stride=CX), :].T
    return jnp.concatenate([t[:HALF], t[HALF:]], axis=1)


def turn_kernel(h_ref, ht_ref):
    for x in range(CX):
        ht_ref[x] = turned(h_ref, x)


def turn_source_kernel(s_ref, ht_ref, st_ref, nlo_ref, nhi_ref):
    low = lanes((8, 128)) < 64
    for x in range(CX):
        s = turned(s_ref, x)
        st_ref[x] = s
        nlo_ref[x] = jnp.where(low, swap(ht_ref[x, HALF - 8 :]), s[HALF - 8 :])
        nhi_ref[x] = jnp.where(low, ht_ref[x, :8], swap(s[:8]))


def cond_kernel(modes_ref, out_ref, work_ref, xrow_ref):
    start_x = lax.axis_index("east") * CX - WIDE
    start_y = lax.axis_index("north") * CY - 8
    exact = dict(precision=lax.Precision.HIGHEST, preferred_element_type=F32)
    ca = lax.broadcasted_iota(jnp.int32, (64, 8), 0)
    order_c, order_a, order_b = (ca // 8).astype(F32), (ca % 8).astype(F32), lanes((64, 8)).astype(F32)
    spectrum = 1.0 / (1.0 + (order_c * order_c + order_a * order_a + order_b * order_b) / 4.0)
    total = jnp.sum(jnp.sum(spectrum, axis=1, keepdims=True), axis=0, keepdims=True)
    weights = modes_ref[...] * jnp.sqrt(spectrum) * (1.0 / jnp.sqrt(total))
    row = lax.broadcasted_iota(jnp.int32, (ROWS, 8), 0)
    order = lanes((ROWS, 8)).astype(F32)
    halves = []
    for half in range(2):
        coord = (start_y + half * HALF + row).astype(F32) + 0.5
        table = jnp.cos(jnp.pi * order * coord / NY)
        halves.append(lax.dot_general(table, weights, (((1,), (1,)), ((), ())), **exact))
    base = jnp.concatenate(halves, axis=1)
    x = start_x + lax.broadcasted_iota(jnp.int32, (32, 128), 0)
    order = (lanes((32, 128)) % 8).astype(F32)
    xrow_ref[...] = jnp.cos(jnp.pi * order * (x.astype(F32) + 0.5) / NX)
    lane_z = lanes((128, 128))
    mode = lax.broadcasted_iota(jnp.int32, (128, 128), 0)
    order = ((mode % 64) // 8).astype(F32)
    table = jnp.cos(jnp.pi * order * ((lane_z % 64).astype(F32) + 0.5) / LZ)
    table = jnp.where(mode // 64 == lane_z // 64, table, 0.0)
    lane = lanes((ROWS, 128))
    y = start_y + lax.broadcasted_iota(jnp.int32, (ROWS, 128), 0) + (lane // 64) * HALF
    inside_y = one((y >= 0) & (y < NY))
    for first in range(0, EXT, EXT // 2):
        for i in range(EXT // 2):
            work_ref[i * ROWS : (i + 1) * ROWS] = base * xrow_ref[first + i : first + i + 1, :]
        log = jnp.dot(work_ref[...], table, **exact)
        for i in range(EXT // 2):
            xg = start_x + first + i
            live = inside_y * one((xg >= 0) & (xg < NX))
            value = jnp.exp(log[i * ROWS : (i + 1) * ROWS])
            out_ref[first + i] = jnp.where(live > 0.0, 0.5 * value, 0.0)


def rel(h):
    return jnp.exp(jnp.minimum(h, 0.0))


def one(condition):
    return condition.astype(F32)


def split(ref, at, value):
    big = value.astype(jnp.bfloat16)
    ref[at, 0:128] = big
    ref[at, 128:256] = (value - big.astype(F32)).astype(jnp.bfloat16)


def edges():
    z = lanes((8, 128)) % 64
    return one(z < LZ - 1), one(z > 0)


def grid_tables(count_ref, mask_ref):
    north = lax.axis_index("north")
    lane = lanes((ROWS, 128))
    y = north * CY - 8 + lax.broadcasted_iota(jnp.int32, (ROWS, 128), 0) + (lane // 64) * HALF
    z = lane % 64
    count_ref[...] = one(y > 0) + one(y < NY - 1) + one(z > 0) + one(z < LZ - 1)
    mask_ref[...] = one((y >= 0) & (y < NY))


def clear_pads(refs):
    zero = jnp.zeros((8, 128), F32)
    for ref in refs:
        for i in range(ref.shape[0]):
            ref[i, 0:8] = zero
            ref[i, PAD - 8 : PAD] = zero


def start_row(at, h, s, nlo, nhi, cond, ha, ka, sto_ref, src_ref):
    low = lanes((8, 128)) < 64
    north = lax.axis_index("north")
    nlo = jnp.where(north > 0, nlo, 0.0)
    nhi = jnp.where(north < 15, nhi, 0.0)
    pieces = [(0, jnp.where(low, nlo, swap(h[HALF - 8 :])))]
    pieces += [(8 + r, h[r : r + 8]) for r in range(0, HALF, 8)]
    pieces += [(ROWS - 8, swap(jnp.where(low, nhi, h[:8])))]
    if s is not None:
        sources = [swap(jnp.where(low, s[HALF - 8 :], nlo))]
        sources += [s[r : r + 8] for r in range(0, HALF, 8)]
        sources += [jnp.where(low, swap(s[:8]), nhi)]
    for n, (r, piece) in enumerate(pieces):
        relative = rel(piece)
        ha[at, 4 + r : 12 + r] = piece
        ka[at, 4 + r : 12 + r] = cond(r) * relative
        if s is not None:
            sto = 0.5 + 0.5 * relative
            sto_ref[at, r : r + 8] = sto
            src_ref[at, r : r + 8] = sto * piece + sources[n]


def sweep_row(at, xi, hin, kin, hout, kout, cond_ref, sto_ref, src_ref, count_ref, mask_ref):
    up_mask, down_mask = edges()
    gravity = up_mask - down_mask
    xg = lax.axis_index("east") * CX - WIDE + xi
    along_x = one(xg > 0) + one(xg < NX - 1)
    in_x = one((xg >= 0) & (xg < NX))
    for a in range(8, PAD - 8, 8):
        r = a - 4
        h, k = hin[at, a : a + 8], kin[at, a : a + 8]
        hu = pltpu.roll(h, 127, 1) * up_mask
        ku = pltpu.roll(k, 127, 1) * up_mask
        hd = pltpu.roll(h, 1, 1) * down_mask
        kd = pltpu.roll(k, 1, 1) * down_mask
        hn, kn = hin[at, a + 1 : a + 9], kin[at, a + 1 : a + 9]
        hs, ks = hin[at, a - 1 : a + 7], kin[at, a - 1 : a + 7]
        he, ke = hin[at + 1, a : a + 8], kin[at + 1, a : a + 8]
        hw, kw = hin[at - 1, a : a + 8], kin[at - 1, a : a + 8]
        sum_h = ((hu + hd) + (hn + hs)) + ((he + hw) + gravity)
        sum_k = ((ku + kd) + (kn + ks)) + (ke + kw)
        flux = ((ku * hu + kd * hd) + (kn * hn + ks * hs)) + (ke * he + kw * hw)
        top = (src_ref[at, r : r + 8] + k * sum_h) + (flux + (ku - kd))
        below = (count_ref[r : r + 8] + along_x) * k + (sto_ref[at, r : r + 8] + sum_k)
        inv = pltpu.reciprocal(below, approx=True)
        inv = inv * (2.0 - below * inv)
        inv = inv * (2.0 - below * inv)
        new = top * inv * in_x
        if a == 8 or a == PAD - 16:
            new = new * mask_ref[r : r + 8]
        hout[at, a : a + 8] = new
        kout[at, a : a + 8] = cond_ref[xi, r : r + 8] * rel(new)


def velocity_row(at, row, size, h_ref, k_ref, table_ref):
    up_mask, down_mask = edges()
    up_mask = jnp.concatenate([up_mask, up_mask], axis=0)
    down_mask = jnp.concatenate([down_mask, down_mask], axis=0)
    for r in range(0, HALF, 16):
        a = r + 12
        h, k = h_ref[at, a : a + 16], k_ref[at, a : a + 16]
        hu = pltpu.roll(h, 127, 1) * up_mask
        hd = pltpu.roll(h, 1, 1) * down_mask
        flow_x = -k * (h_ref[at + 1, a : a + 16] - h_ref[at - 1, a : a + 16])
        flow_y = -k * (h_ref[at, a + 1 : a + 17] - h_ref[at, a - 1 : a + 15])
        flow_z = -k * ((hu - hd) + 2.0)
        for c, flow in enumerate((flow_x, flow_y, flow_z)):
            split(table_ref, pl.ds(pl.multiple_of(row + c * size + r, 16), 16), flow)


def own_row(x, at, ht_ref, st_ref, nlo_ref, nhi_ref, cond_ref, ha, ka, sto_ref, src_ref):
    cond = lambda r: cond_ref[x + WIDE, r : r + 8]
    start_row(at, ht_ref[x], st_ref[x], nlo_ref[x], nhi_ref[x], cond, ha, ka, sto_ref, src_ref)


def edge_kernel(
    ht_ref, st_ref, nlo_ref, nhi_ref, cond_ref, up_ref, down_ref,
    ha, hb, ka, kb, sto_ref, src_ref, count_ref, mask_ref,
):
    grid_tables(count_ref, mask_ref)
    clear_pads((hb, kb))
    tables = (cond_ref, sto_ref, src_ref, count_ref, mask_ref)
    for send_ref, first_x, a, b in ((up_ref, CX - WIDE, WIDE - 1, WIDE - 2), (down_ref, 0, 0, 1)):

        def own(at, carry, first_x=first_x):
            own_row(first_x + at, at, ht_ref, st_ref, nlo_ref, nhi_ref, cond_ref, ha, ka, sto_ref, src_ref)
            return carry

        lax.fori_loop(0, WIDE, own, 0)

        def sweep(at, carry, first_x=first_x):
            sweep_row(at, WIDE + first_x + at, ha, ka, hb, kb, *tables)
            return carry

        lax.fori_loop(1, 4, sweep, 0)
        sweep_row(2, WIDE + first_x + 2, hb, kb, ha, ka, *tables)
        parts = ((ha, a, 8), (ha, b, 8), (src_ref, a, 4), (src_ref, b, 4), (hb, b, 8), (hb, 2, 8), (ha, 2, 8))
        for n, (source, at, r) in enumerate(parts):
            send_ref[n * SPAN : (n + 1) * SPAN] = source[at, r : r + SPAN]


def inner_kernel(
    ht_ref, st_ref, nlo_ref, nhi_ref, cond_ref,
    ha, hb, ka, kb, sto_ref, src_ref, table_ref,
    count_ref, mask_ref,
):
    grid_tables(count_ref, mask_ref)
    clear_pads((hb, kb))

    def own(x, carry):
        cond = lambda r: cond_ref[x + WIDE, r : r + 8]
        start_row(x, ht_ref[x], st_ref[x], nlo_ref[x], nhi_ref[x], cond, ha, ka, sto_ref, src_ref)
        return carry

    lax.fori_loop(0, CX, own, 0)
    hin, kin, hout, kout = ha, ka, hb, kb
    for number in range(1, ITERS + 1):

        def sweep(x, carry, hin=hin, kin=kin, hout=hout, kout=kout):
            sweep_row(x, x + WIDE, hin, kin, hout, kout, cond_ref, sto_ref, src_ref, count_ref, mask_ref)
            return carry

        lax.fori_loop(number, CX - number, sweep, 0)
        hin, kin, hout, kout = hout, kout, hin, kin

    def velocity(i, carry):
        velocity_row(i + WIDE, i * HALF, MID * HALF, hin, kin, table_ref)
        return carry

    lax.fori_loop(0, MID, velocity, 0)


def outer_kernel(
    ha0, hb0, ka0, kb0, sto0, src0, elo_ref, ehi_ref, cond_ref,
    heads_ref, table_ref,
    ha, hb, ka, kb, sto_ref, src_ref, count_ref, mask_ref,
):
    east = lax.axis_index("east")
    grid_tables(count_ref, mask_ref)
    clear_pads((ha, hb, ka, kb))
    for x in range(CX):
        depth = min(x, CX - 1 - x)
        if depth <= WIDE:
            ha[x + WIDE], ka[x + WIDE] = ha0[x], ka0[x]
        if 1 <= depth <= ITERS:
            hb[x + WIDE], kb[x + WIDE] = hb0[x], kb0[x]
    for small, big in ((sto0, sto_ref), (src0, src_ref)):
        for i in range(ITERS):
            big[WIDE + i] = small[i]
            big[EXT - 1 - WIDE - i] = small[CX - 1 - i]
    for ref, valid, near, out in ((elo_ref, east > 0, WIDE - 1, -1), (ehi_ref, east < 15, EXT - WIDE, 1)):
        block = lambda n, ref=ref, valid=valid: jnp.where(valid, ref[n * SPAN : (n + 1) * SPAN], 0.0)
        for n, big_h, big_k, depth in ((0, ha, ka, 0), (1, ha, ka, 1), (4, hb, kb, 1), (5, hb, kb, 2), (6, ha, ka, 2)):
            xi = near + out * depth
            h = block(n)
            relative = rel(h)
            big_h[xi, 8 : 8 + SPAN] = h
            big_k[xi, 8 : 8 + SPAN] = cond_ref[xi, 4 : 4 + SPAN] * relative
            if n < 2:
                sto_ref[xi, 4 : 4 + SPAN] = 0.5 + 0.5 * relative
                src_ref[xi, 4 : 4 + SPAN] = block(n + 2)

    hin, kin, hout, kout = ha, ka, hb, kb
    for first, count in ((4, 2), (3, 4), (3, 5), (4, 5)):

        def sweep(i, carry, first=first, count=count, hin=hin, kin=kin, hout=hout, kout=kout):
            xi = jnp.where(i < count, first + i, EXT - 1 - first - (i - count))
            sweep_row(xi, xi, hin, kin, hout, kout, cond_ref, sto_ref, src_ref, count_ref, mask_ref)
            return carry

        lax.fori_loop(0, 2 * count, sweep, 0)
        hin, kin, hout, kout = hout, kout, hin, kin

    for x in range(CX):
        source, at = (ha0, x) if WIDE <= x < CX - WIDE else (hin, x + WIDE)
        heads_ref[x] = source[at, 12 : 12 + HALF]

    def velocity(i, carry):
        at = i + WIDE + jnp.where(i < WIDE, 0, MID)
        velocity_row(at, i * HALF, OUT * HALF, hin, kin, table_ref)
        return carry

    lax.fori_loop(0, OUT, velocity, 0)


def onehot_pair(index):
    hot = lax.broadcasted_iota(jnp.int32, (128, index.shape[1]), 0) == index
    hot = jnp.where(hot, 1.0, 0.0).astype(jnp.bfloat16)
    return jnp.concatenate([hot, hot], axis=0)


def choose(get, first, count, bits):
    if count == 1:
        return get(first)
    level = (count - 1).bit_length() - 1
    half = 1 << level
    low = choose(get, first, half, bits)
    high = choose(get, first + half, count - half, bits)
    return jnp.where(bits[level], high, low)


BLOCK = 512
PARTS = BLOCK // 128


def read_cells(cell_ref, n):
    cell = jnp.concatenate([cell_ref[pl.ds(n * PARTS + i, 1), :] for i in range(PARTS)], axis=1)
    layer, x, j = cell >> 11, (cell >> 7) & 15, cell & 127
    return x, j & 63, (j >> 6) * 64 + layer


def sampled_at(table_ref, count, place, inner_y, lane):
    got = jnp.dot(table_ref[...], onehot_pair(lane), preferred_element_type=F32)
    row8 = jnp.broadcast_to(place * 64 + inner_y, (8, BLOCK))
    bits = [(row8 & (8 << b)) != 0 for b in range(7)]
    mine = lax.broadcasted_iota(jnp.int32, (8, BLOCK), 0) == (row8 & 7)
    size = count * HALF
    for c in range(3):
        picked = choose(lambda g: got[c * size + g * 8 : c * size + g * 8 + 8], 0, count * 8, bits)
        yield c, jnp.sum(jnp.where(mine, picked, 0.0), axis=0, keepdims=True)


def sample_inner_kernel(table_ref, cell_ref, part_ref):
    def block(n, carry):
        x, inner_y, lane = read_cells(cell_ref, n)
        at = pl.ds(pl.multiple_of(n * BLOCK, BLOCK), BLOCK)
        for c, sampled in sampled_at(table_ref, MID, jnp.clip(x - WIDE, 0, MID - 1), inner_y, lane):
            part_ref[c : c + 1, at] = sampled
        return carry

    lax.fori_loop(0, 4096 // BLOCK, block, 0, unroll=4)


def sample_kernel(
    table_ref, cell_ref, part_ref, rec_ref, couple_ref, list_ref, count_ref, moved_ref, send_ref, pick_ref
):
    def block(n, carry):
        x, inner_y, lane = read_cells(cell_ref, n)
        middle = (x >= WIDE) & (x < CX - WIDE)
        place = jnp.where(x < WIDE, x, jnp.maximum(x - MID, 0))
        at = pl.ds(pl.multiple_of(n * BLOCK, BLOCK), BLOCK)
        total = rec_ref[:, at]
        for c, outer in sampled_at(table_ref, OUT, place, inner_y, lane):
            sampled = jnp.where(middle, part_ref[c : c + 1, at], outer)
            weight = couple_ref[c * 32 : (c + 1) * 32, :]
            total = total + jnp.concatenate([weight] * PARTS, axis=1) * sampled
        moved_ref[:, at] = total
        for i in range(PARTS):
            rows = pl.ds(pl.multiple_of((n * PARTS + i) * 32, 32), 32)
            split(pick_ref, rows, total[:, i * 128 : (i + 1) * 128])
        return carry

    lax.fori_loop(0, 4096 // BLOCK, block, 0, unroll=4)
    for d in range(4):
        index = list_ref[d : d + 1, :]
        got = jnp.dot(pick_ref[...], onehot_pair(index & 127), preferred_element_type=F32)
        block_of = jnp.broadcast_to(index >> 7, (32, BLOCK))
        bits = [(block_of & (1 << b)) != 0 for b in range(5)]
        picked = choose(lambda g: got[g * 32 : (g + 1) * 32], 0, 32, bits)
        live = lanes((32, BLOCK)) < count_ref[d, 0]
        send_ref[d] = jnp.where(live, picked, 0.0)


def back_kernel(ht_ref, out_ref):
    for x in range(CX):
        t = ht_ref[x].T
        out_ref[pl.ds(x, LZ, stride=CX), :] = jnp.concatenate([t[:LZ], t[LZ:]], axis=1)


def arrive_kernel(a_ref, b_ref, c_ref, d_ref, out_ref):
    east, north = lax.axis_index("east"), lax.axis_index("north")
    for d, (ref, valid) in enumerate(
        ((a_ref, east > 0), (b_ref, east < 15), (c_ref, north > 0), (d_ref, north < 15))
    ):
        out_ref[d] = jnp.where(valid, ref[...], 0.0)


def call(kernel, outs, ins, scratch=(), limit=6, specs=None):
    return pl.pallas_call(
        kernel,
        out_shape=[jax.ShapeDtypeStruct(s, t) for s, t in outs],
        in_specs=specs or [VMEM] * len(ins),
        out_specs=[VMEM] * len(outs),
        scratch_shapes=list(scratch),
        compiler_params=pltpu.CompilerParams(vmem_limit_bytes=limit * 2**20),
    )(*ins)


def ring(value, axis, steps):
    count = lax.axis_size(axis)
    return lax.ppermute(value, axis, [(i, (i + steps) % count) for i in range(count)])


def on_device(head_old, source, mode_coeffs, records, cell_index, coupling, send_list, send_count):
    flat = (LZ * CX, CY)
    tile = ((CX, HALF, 128), F32)
    side = ((CX, 8, 128), F32)
    (ht,) = call(turn_kernel, [tile], [head_old.reshape(flat)])
    st, n_up, n_down = call(turn_source_kernel, [tile, side, side], [source.reshape(flat), ht])
    nlo = ring(n_up, "north", 1)
    nhi = ring(n_down, "north", -1)
    (cond,) = call(
        cond_kernel,
        [((EXT, ROWS, 128), F32)],
        [mode_coeffs.reshape(64, 8)],
        [pltpu.VMEM((EXT // 2 * ROWS, 128), F32), pltpu.VMEM((32, 128), F32)],
        limit=12,
    )
    nlo, nhi, cond = lax.optimization_barrier((nlo, nhi, cond))
    edge = ((ESEND, 128), F32)
    plane = pltpu.VMEM((ROWS, 128), F32)
    some, some_base = pltpu.VMEM((WIDE, PAD, 128), F32), pltpu.VMEM((WIDE, ROWS, 128), F32)
    e_up, e_down = call(
        edge_kernel,
        [edge, edge],
        [ht, st, nlo, nhi, cond],
        [some] * 4 + [some_base] * 2 + [plane, plane],
        limit=8,
    )
    elo = ring(e_up, "east", 1)
    ehi = ring(e_down, "east", -1)
    level = ((CX, PAD, 128), F32)
    base = ((CX, ROWS, 128), F32)
    cells = cell_index.reshape(32, 128)
    *inner, table_mid = call(
        inner_kernel,
        [level] * 4 + [base] * 2 + [((3 * MID * HALF, 256), jnp.bfloat16)],
        [ht, st, nlo, nhi, cond],
        [plane, plane],
        limit=12,
    )
    (part,) = call(sample_inner_kernel, [((8, 4096), F32)], [table_mid, cells], limit=20)
    buf = pltpu.VMEM((EXT, PAD, 128), F32)
    ext = pltpu.VMEM((EXT, ROWS, 128), F32)
    heads, table = call(
        outer_kernel,
        [tile, ((3 * OUT * HALF, 256), jnp.bfloat16)],
        list(inner) + [elo, ehi, cond],
        [buf, buf, buf, buf, ext, ext, plane, plane],
        limit=20,
    )
    couple = jnp.broadcast_to((STEP * coupling)[:, :, None], (3, 32, 128)).reshape(96, 128)
    moved, buffers = call(
        sample_kernel,
        [((32, 4096), F32), ((4, 32, 512), F32)],
        [table, cells, part, records, couple, send_list, send_count],
        [pltpu.VMEM((1024, 256), jnp.bfloat16)],
        limit=32,
        specs=[VMEM] * 6 + [SMEM],
    )
    came = [
        ring(buffers[0], "east", 1),
        ring(buffers[1], "east", -1),
        ring(buffers[2], "north", 1),
        ring(buffers[3], "north", -1),
    ]
    (heads_out,) = call(back_kernel, [(flat, F32)], [heads])
    (arrivals,) = call(arrive_kernel, [((4, 32, 512), F32)], came)
    return (heads_out.reshape(LZ, CX, CY), moved, arrivals)


def solution(mesh):
    return jax.shard_map(
        on_device,
        mesh=mesh,
        in_specs=(
            P(None, "east", "north"),
            P(None, "east", "north"),
            P(),
            P(None, ("east", "north")),
            P(("east", "north")),
            P(),
            P(None, ("east", "north")),
            P(None, ("east", "north")),
        ),
        out_specs=(
            P(None, "east", "north"),
            P(None, ("east", "north")),
            P(None, None, ("east", "north")),
        ),
        check_vma=False,
    )
```

```python
import jax
import jax.numpy as jnp
from jax import lax
from jax.experimental import pallas as pl
from jax.experimental.pallas import tpu as pltpu
from jax.sharding import PartitionSpec as P

ITERS = 4
LZ, CX, CY = 64, 16, 128
HALF = CY // 2
WIDE = ITERS + 1
EXT = CX + 2 * WIDE
ROWS = HALF + 16
PAD = ROWS + 8
MID = CX - 2 * WIDE
OUT = CX - MID
NX, NY = 256, 2048
SPAN = HALF + 8
ESEND = 7 * SPAN
STEP = 0.25
F32 = jnp.float32
VMEM = pl.BlockSpec(memory_space=pltpu.VMEM)
SMEM = pl.BlockSpec(memory_space=pltpu.SMEM)


def lanes(shape):
    return lax.broadcasted_iota(jnp.int32, shape, len(shape) - 1)


def swap(v):
    return pltpu.roll(v, 64, 1)


def turned(ref, x):
    t = ref[pl.ds(x, LZ, stride=CX), :].T
    return jnp.concatenate([t[:HALF], t[HALF:]], axis=1)


def turn_kernel(h_ref, ht_ref):
    for x in range(CX):
        ht_ref[x] = turned(h_ref, x)


def turn_source_kernel(s_ref, ht_ref, st_ref, nlo_ref, nhi_ref):
    low = lanes((8, 128)) < 64
    for x in range(CX):
        s = turned(s_ref, x)
        st_ref[x] = s
        nlo_ref[x] = jnp.where(low, swap(ht_ref[x, HALF - 8 :]), s[HALF - 8 :])
        nhi_ref[x] = jnp.where(low, ht_ref[x, :8], swap(s[:8]))


def cond_kernel(modes_ref, out_ref, work_ref, xrow_ref):
    start_x = lax.axis_index("east") * CX - WIDE
    start_y = lax.axis_index("north") * CY - 8
    exact = dict(precision=lax.Precision.HIGHEST, preferred_element_type=F32)
    ca = lax.broadcasted_iota(jnp.int32, (64, 8), 0)
    order_c, order_a, order_b = (ca // 8).astype(F32), (ca % 8).astype(F32), lanes((64, 8)).astype(F32)
    spectrum = 1.0 / (1.0 + (order_c * order_c + order_a * order_a + order_b * order_b) / 4.0)
    total = jnp.sum(jnp.sum(spectrum, axis=1, keepdims=True), axis=0, keepdims=True)
    weights = modes_ref[...] * jnp.sqrt(spectrum) * (1.0 / jnp.sqrt(total))
    row = lax.broadcasted_iota(jnp.int32, (ROWS, 8), 0)
    order = lanes((ROWS, 8)).astype(F32)
    halves = []
    for half in range(2):
        coord = (start_y + half * HALF + row).astype(F32) + 0.5
        table = jnp.cos(jnp.pi * order * coord / NY)
        halves.append(lax.dot_general(table, weights, (((1,), (1,)), ((), ())), **exact))
    base = jnp.concatenate(halves, axis=1)
    x = start_x + lax.broadcasted_iota(jnp.int32, (32, 128), 0)
    order = (lanes((32, 128)) % 8).astype(F32)
    xrow_ref[...] = jnp.cos(jnp.pi * order * (x.astype(F32) + 0.5) / NX)
    lane_z = lanes((128, 128))
    mode = lax.broadcasted_iota(jnp.int32, (128, 128), 0)
    order = ((mode % 64) // 8).astype(F32)
    table = jnp.cos(jnp.pi * order * ((lane_z % 64).astype(F32) + 0.5) / LZ)
    table = jnp.where(mode // 64 == lane_z // 64, table, 0.0)
    lane = lanes((ROWS, 128))
    y = start_y + lax.broadcasted_iota(jnp.int32, (ROWS, 128), 0) + (lane // 64) * HALF
    inside_y = one((y >= 0) & (y < NY))
    for first in range(0, EXT, EXT // 2):
        for i in range(EXT // 2):
            work_ref[i * ROWS : (i + 1) * ROWS] = base * xrow_ref[first + i : first + i + 1, :]
        log = jnp.dot(work_ref[...], table, **exact)
        for i in range(EXT // 2):
            xg = start_x + first + i
            live = inside_y * one((xg >= 0) & (xg < NX))
            value = jnp.exp(log[i * ROWS : (i + 1) * ROWS])
            out_ref[first + i] = jnp.where(live > 0.0, 0.5 * value, 0.0)


def rel(h):
    return jnp.exp(jnp.minimum(h, 0.0))


def one(condition):
    return condition.astype(F32)


def split(ref, at, value):
    big = value.astype(jnp.bfloat16)
    ref[at, 0:128] = big
    ref[at, 128:256] = (value - big.astype(F32)).astype(jnp.bfloat16)


def edges():
    z = lanes((8, 128)) % 64
    return one(z < LZ - 1), one(z > 0)


def grid_tables(count_ref, mask_ref):
    north = lax.axis_index("north")
    lane = lanes((ROWS, 128))
    y = north * CY - 8 + lax.broadcasted_iota(jnp.int32, (ROWS, 128), 0) + (lane // 64) * HALF
    z = lane % 64
    count_ref[...] = one(y > 0) + one(y < NY - 1) + one(z > 0) + one(z < LZ - 1)
    mask_ref[...] = one((y >= 0) & (y < NY))


def clear_pads(refs):
    zero = jnp.zeros((8, 128), F32)
    for ref in refs:
        for i in range(ref.shape[0]):
            ref[i, 0:8] = zero
            ref[i, PAD - 8 : PAD] = zero


def start_row(at, h, s, nlo, nhi, cond, ha, ka, sto_ref, src_ref):
    low = lanes((8, 128)) < 64
    north = lax.axis_index("north")
    nlo = jnp.where(north > 0, nlo, 0.0)
    nhi = jnp.where(north < 15, nhi, 0.0)
    pieces = [(0, jnp.where(low, nlo, swap(h[HALF - 8 :])))]
    pieces += [(8 + r, h[r : r + 8]) for r in range(0, HALF, 8)]
    pieces += [(ROWS - 8, swap(jnp.where(low, nhi, h[:8])))]
    if s is not None:
        sources = [swap(jnp.where(low, s[HALF - 8 :], nlo))]
        sources += [s[r : r + 8] for r in range(0, HALF, 8)]
        sources += [jnp.where(low, swap(s[:8]), nhi)]
    for n, (r, piece) in enumerate(pieces):
        relative = rel(piece)
        ha[at, 4 + r : 12 + r] = piece
        ka[at, 4 + r : 12 + r] = cond(r) * relative
        if s is not None:
            sto = 0.5 + 0.5 * relative
            sto_ref[at, r : r + 8] = sto
            src_ref[at, r : r + 8] = sto * piece + sources[n]


def sweep_row(at, xi, hin, kin, hout, kout, cond_ref, sto_ref, src_ref, count_ref, mask_ref):
    up_mask, down_mask = edges()
    gravity = up_mask - down_mask
    xg = lax.axis_index("east") * CX - WIDE + xi
    along_x = one(xg > 0) + one(xg < NX - 1)
    in_x = one((xg >= 0) & (xg < NX))
    for a in range(8, PAD - 8, 8):
        r = a - 4
        h, k = hin[at, a : a + 8], kin[at, a : a + 8]
        hu = pltpu.roll(h, 127, 1) * up_mask
        ku = pltpu.roll(k, 127, 1) * up_mask
        hd = pltpu.roll(h, 1, 1) * down_mask
        kd = pltpu.roll(k, 1, 1) * down_mask
        hn, kn = hin[at, a + 1 : a + 9], kin[at, a + 1 : a + 9]
        hs, ks = hin[at, a - 1 : a + 7], kin[at, a - 1 : a + 7]
        he, ke = hin[at + 1, a : a + 8], kin[at + 1, a : a + 8]
        hw, kw = hin[at - 1, a : a + 8], kin[at - 1, a : a + 8]
        sum_h = ((hu + hd) + (hn + hs)) + ((he + hw) + gravity)
        sum_k = ((ku + kd) + (kn + ks)) + (ke + kw)
        flux = ((ku * hu + kd * hd) + (kn * hn + ks * hs)) + (ke * he + kw * hw)
        top = (src_ref[at, r : r + 8] + k * sum_h) + (flux + (ku - kd))
        below = (count_ref[r : r + 8] + along_x) * k + (sto_ref[at, r : r + 8] + sum_k)
        inv = pltpu.reciprocal(below, approx=True)
        inv = inv * (2.0 - below * inv)
        inv = inv * (2.0 - below * inv)
        new = top * inv * in_x
        if a == 8 or a == PAD - 16:
            new = new * mask_ref[r : r + 8]
        hout[at, a : a + 8] = new
        kout[at, a : a + 8] = cond_ref[xi, r : r + 8] * rel(new)


def velocity_row(at, row, size, h_ref, k_ref, table_ref):
    up_mask, down_mask = edges()
    up_mask = jnp.concatenate([up_mask, up_mask], axis=0)
    down_mask = jnp.concatenate([down_mask, down_mask], axis=0)
    for r in range(0, HALF, 16):
        a = r + 12
        h, k = h_ref[at, a : a + 16], k_ref[at, a : a + 16]
        hu = pltpu.roll(h, 127, 1) * up_mask
        hd = pltpu.roll(h, 1, 1) * down_mask
        flow_x = -k * (h_ref[at + 1, a : a + 16] - h_ref[at - 1, a : a + 16])
        flow_y = -k * (h_ref[at, a + 1 : a + 17] - h_ref[at, a - 1 : a + 15])
        flow_z = -k * ((hu - hd) + 2.0)
        for c, flow in enumerate((flow_x, flow_y, flow_z)):
            split(table_ref, pl.ds(pl.multiple_of(row + c * size + r, 16), 16), flow)


def own_row(x, at, ht_ref, st_ref, nlo_ref, nhi_ref, cond_ref, ha, ka, sto_ref, src_ref):
    cond = lambda r: cond_ref[x + WIDE, r : r + 8]
    start_row(at, ht_ref[x], st_ref[x], nlo_ref[x], nhi_ref[x], cond, ha, ka, sto_ref, src_ref)


def edge_kernel(
    ht_ref, st_ref, nlo_ref, nhi_ref, cond_ref, up_ref, down_ref,
    ha, hb, ka, kb, sto_ref, src_ref, count_ref, mask_ref,
):
    grid_tables(count_ref, mask_ref)
    clear_pads((hb, kb))
    tables = (cond_ref, sto_ref, src_ref, count_ref, mask_ref)
    for send_ref, first_x, a, b in ((up_ref, CX - WIDE, WIDE - 1, WIDE - 2), (down_ref, 0, 0, 1)):

        def own(at, carry, first_x=first_x):
            own_row(first_x + at, at, ht_ref, st_ref, nlo_ref, nhi_ref, cond_ref, ha, ka, sto_ref, src_ref)
            return carry

        lax.fori_loop(0, WIDE, own, 0)

        def sweep(at, carry, first_x=first_x):
            sweep_row(at, WIDE + first_x + at, ha, ka, hb, kb, *tables)
            return carry

        lax.fori_loop(1, 4, sweep, 0)
        sweep_row(2, WIDE + first_x + 2, hb, kb, ha, ka, *tables)
        parts = ((ha, a, 8), (ha, b, 8), (src_ref, a, 4), (src_ref, b, 4), (hb, b, 8), (hb, 2, 8), (ha, 2, 8))
        for n, (source, at, r) in enumerate(parts):
            send_ref[n * SPAN : (n + 1) * SPAN] = source[at, r : r + SPAN]


def inner_kernel(
    ht_ref, st_ref, nlo_ref, nhi_ref, cond_ref,
    ha, hb, ka, kb, sto_ref, src_ref, table_ref,
    count_ref, mask_ref,
):
    grid_tables(count_ref, mask_ref)
    clear_pads((hb, kb))

    def own(x, carry):
        cond = lambda r: cond_ref[x + WIDE, r : r + 8]
        start_row(x, ht_ref[x], st_ref[x], nlo_ref[x], nhi_ref[x], cond, ha, ka, sto_ref, src_ref)
        return carry

    lax.fori_loop(0, CX, own, 0)
    hin, kin, hout, kout = ha, ka, hb, kb
    for number in range(1, ITERS + 1):

        def sweep(x, carry, hin=hin, kin=kin, hout=hout, kout=kout):
            sweep_row(x, x + WIDE, hin, kin, hout, kout, cond_ref, sto_ref, src_ref, count_ref, mask_ref)
            return carry

        lax.fori_loop(number, CX - number, sweep, 0)
        hin, kin, hout, kout = hout, kout, hin, kin

    def velocity(i, carry):
        velocity_row(i + WIDE, i * HALF, MID * HALF, hin, kin, table_ref)
        return carry

    lax.fori_loop(0, MID, velocity, 0)


def outer_kernel(
    ha0, hb0, ka0, kb0, sto0, src0, elo_ref, ehi_ref, cond_ref,
    heads_ref, table_ref,
    ha, hb, ka, kb, sto_ref, src_ref, count_ref, mask_ref,
):
    east = lax.axis_index("east")
    grid_tables(count_ref, mask_ref)
    clear_pads((ha, hb, ka, kb))
    for x in range(CX):
        depth = min(x, CX - 1 - x)
        if depth <= WIDE:
            ha[x + WIDE], ka[x + WIDE] = ha0[x], ka0[x]
        if 1 <= depth <= ITERS:
            hb[x + WIDE], kb[x + WIDE] = hb0[x], kb0[x]
    for small, big in ((sto0, sto_ref), (src0, src_ref)):
        for i in range(ITERS):
            big[WIDE + i] = small[i]
            big[EXT - 1 - WIDE - i] = small[CX - 1 - i]
    for ref, valid, near, out in ((elo_ref, east > 0, WIDE - 1, -1), (ehi_ref, east < 15, EXT - WIDE, 1)):
        block = lambda n, ref=ref, valid=valid: jnp.where(valid, ref[n * SPAN : (n + 1) * SPAN], 0.0)
        for n, big_h, big_k, depth in ((0, ha, ka, 0), (1, ha, ka, 1), (4, hb, kb, 1), (5, hb, kb, 2), (6, ha, ka, 2)):
            xi = near + out * depth
            h = block(n)
            relative = rel(h)
            big_h[xi, 8 : 8 + SPAN] = h
            big_k[xi, 8 : 8 + SPAN] = cond_ref[xi, 4 : 4 + SPAN] * relative
            if n < 2:
                sto_ref[xi, 4 : 4 + SPAN] = 0.5 + 0.5 * relative
                src_ref[xi, 4 : 4 + SPAN] = block(n + 2)

    hin, kin, hout, kout = ha, ka, hb, kb
    for first, count in ((4, 2), (3, 4), (3, 5), (4, 5)):

        def sweep(i, carry, first=first, count=count, hin=hin, kin=kin, hout=hout, kout=kout):
            xi = jnp.where(i < count, first + i, EXT - 1 - first - (i - count))
            sweep_row(xi, xi, hin, kin, hout, kout, cond_ref, sto_ref, src_ref, count_ref, mask_ref)
            return carry

        lax.fori_loop(0, 2 * count, sweep, 0)
        hin, kin, hout, kout = hout, kout, hin, kin

    for x in range(CX):
        source, at = (ha0, x) if WIDE <= x < CX - WIDE else (hin, x + WIDE)
        heads_ref[x] = source[at, 12 : 12 + HALF]

    def velocity(i, carry):
        at = i + WIDE + jnp.where(i < WIDE, 0, MID)
        velocity_row(at, i * HALF, OUT * HALF, hin, kin, table_ref)
        return carry

    lax.fori_loop(0, OUT, velocity, 0)


def onehot_pair(index):
    hot = lax.broadcasted_iota(jnp.int32, (128, index.shape[1]), 0) == index
    hot = jnp.where(hot, 1.0, 0.0).astype(jnp.bfloat16)
    return jnp.concatenate([hot, hot], axis=0)


def choose(get, first, count, bits):
    if count == 1:
        return get(first)
    level = (count - 1).bit_length() - 1
    half = 1 << level
    low = choose(get, first, half, bits)
    high = choose(get, first + half, count - half, bits)
    return jnp.where(bits[level], high, low)


BLOCK = 512
PARTS = BLOCK // 128


def read_cells(cell_ref, n):
    cell = jnp.concatenate([cell_ref[pl.ds(n * PARTS + i, 1), :] for i in range(PARTS)], axis=1)
    layer, x, j = cell >> 11, (cell >> 7) & 15, cell & 127
    return x, j & 63, (j >> 6) * 64 + layer


def sampled_at(table_ref, count, place, inner_y, lane):
    got = jnp.dot(table_ref[...], onehot_pair(lane), preferred_element_type=F32)
    row8 = jnp.broadcast_to(place * 64 + inner_y, (8, BLOCK))
    bits = [(row8 & (8 << b)) != 0 for b in range(7)]
    mine = lax.broadcasted_iota(jnp.int32, (8, BLOCK), 0) == (row8 & 7)
    size = count * HALF
    for c in range(3):
        picked = choose(lambda g: got[c * size + g * 8 : c * size + g * 8 + 8], 0, count * 8, bits)
        yield c, jnp.sum(jnp.where(mine, picked, 0.0), axis=0, keepdims=True)


def sample_inner_kernel(table_ref, cell_ref, part_ref):
    def block(n, carry):
        x, inner_y, lane = read_cells(cell_ref, n)
        at = pl.ds(pl.multiple_of(n * BLOCK, BLOCK), BLOCK)
        for c, sampled in sampled_at(table_ref, MID, jnp.clip(x - WIDE, 0, MID - 1), inner_y, lane):
            part_ref[c : c + 1, at] = sampled
        return carry

    lax.fori_loop(0, 4096 // BLOCK, block, 0, unroll=8)


def sample_kernel(
    table_ref, cell_ref, part_ref, rec_ref, couple_ref, list_ref, count_ref, moved_ref, send_ref, pick_ref
):
    def block(n, carry):
        x, inner_y, lane = read_cells(cell_ref, n)
        middle = (x >= WIDE) & (x < CX - WIDE)
        place = jnp.where(x < WIDE, x, jnp.maximum(x - MID, 0))
        at = pl.ds(pl.multiple_of(n * BLOCK, BLOCK), BLOCK)
        total = rec_ref[:, at]
        for c, outer in sampled_at(table_ref, OUT, place, inner_y, lane):
            sampled = jnp.where(middle, part_ref[c : c + 1, at], outer)
            weight = couple_ref[c * 32 : (c + 1) * 32, :]
            total = total + jnp.concatenate([weight] * PARTS, axis=1) * sampled
        moved_ref[:, at] = total
        for i in range(PARTS):
            rows = pl.ds(pl.multiple_of((n * PARTS + i) * 32, 32), 32)
            split(pick_ref, rows, total[:, i * 128 : (i + 1) * 128])
        return carry

    lax.fori_loop(0, 4096 // BLOCK, block, 0, unroll=8)
    for d in range(4):
        index = list_ref[d : d + 1, :]
        got = jnp.dot(pick_ref[...], onehot_pair(index & 127), preferred_element_type=F32)
        block_of = jnp.broadcast_to(index >> 7, (32, BLOCK))
        bits = [(block_of & (1 << b)) != 0 for b in range(5)]
        picked = choose(lambda g: got[g * 32 : (g + 1) * 32], 0, 32, bits)
        live = lanes((32, BLOCK)) < count_ref[d, 0]
        send_ref[d] = jnp.where(live, picked, 0.0)


def back_kernel(ht_ref, out_ref):
    for x in range(CX):
        t = ht_ref[x].T
        out_ref[pl.ds(x, LZ, stride=CX), :] = jnp.concatenate([t[:LZ], t[LZ:]], axis=1)


def arrive_kernel(a_ref, b_ref, c_ref, d_ref, out_ref):
    east, north = lax.axis_index("east"), lax.axis_index("north")
    for d, (ref, valid) in enumerate(
        ((a_ref, east > 0), (b_ref, east < 15), (c_ref, north > 0), (d_ref, north < 15))
    ):
        out_ref[d] = jnp.where(valid, ref[...], 0.0)


def call(kernel, outs, ins, scratch=(), limit=6, specs=None):
    return pl.pallas_call(
        kernel,
        out_shape=[jax.ShapeDtypeStruct(s, t) for s, t in outs],
        in_specs=specs or [VMEM] * len(ins),
        out_specs=[VMEM] * len(outs),
        scratch_shapes=list(scratch),
        compiler_params=pltpu.CompilerParams(vmem_limit_bytes=limit * 2**20),
    )(*ins)


def ring(value, axis, steps):
    count = lax.axis_size(axis)
    return lax.ppermute(value, axis, [(i, (i + steps) % count) for i in range(count)])


def on_device(head_old, source, mode_coeffs, records, cell_index, coupling, send_list, send_count):
    flat = (LZ * CX, CY)
    tile = ((CX, HALF, 128), F32)
    side = ((CX, 8, 128), F32)
    (ht,) = call(turn_kernel, [tile], [head_old.reshape(flat)])
    st, n_up, n_down = call(turn_source_kernel, [tile, side, side], [source.reshape(flat), ht])
    nlo = ring(n_up, "north", 1)
    nhi = ring(n_down, "north", -1)
    (cond,) = call(
        cond_kernel,
        [((EXT, ROWS, 128), F32)],
        [mode_coeffs.reshape(64, 8)],
        [pltpu.VMEM((EXT // 2 * ROWS, 128), F32), pltpu.VMEM((32, 128), F32)],
        limit=12,
    )
    nlo, nhi, cond = lax.optimization_barrier((nlo, nhi, cond))
    edge = ((ESEND, 128), F32)
    plane = pltpu.VMEM((ROWS, 128), F32)
    some, some_base = pltpu.VMEM((WIDE, PAD, 128), F32), pltpu.VMEM((WIDE, ROWS, 128), F32)
    e_up, e_down = call(
        edge_kernel,
        [edge, edge],
        [ht, st, nlo, nhi, cond],
        [some] * 4 + [some_base] * 2 + [plane, plane],
        limit=8,
    )
    elo = ring(e_up, "east", 1)
    ehi = ring(e_down, "east", -1)
    level = ((CX, PAD, 128), F32)
    base = ((CX, ROWS, 128), F32)
    cells = cell_index.reshape(32, 128)
    *inner, table_mid = call(
        inner_kernel,
        [level] * 4 + [base] * 2 + [((3 * MID * HALF, 256), jnp.bfloat16)],
        [ht, st, nlo, nhi, cond],
        [plane, plane],
        limit=12,
    )
    (part,) = call(sample_inner_kernel, [((8, 4096), F32)], [table_mid, cells], limit=20)
    buf = pltpu.VMEM((EXT, PAD, 128), F32)
    ext = pltpu.VMEM((EXT, ROWS, 128), F32)
    heads, table = call(
        outer_kernel,
        [tile, ((3 * OUT * HALF, 256), jnp.bfloat16)],
        list(inner) + [elo, ehi, cond],
        [buf, buf, buf, buf, ext, ext, plane, plane],
        limit=20,
    )
    couple = jnp.broadcast_to((STEP * coupling)[:, :, None], (3, 32, 128)).reshape(96, 128)
    moved, buffers = call(
        sample_kernel,
        [((32, 4096), F32), ((4, 32, 512), F32)],
        [table, cells, part, records, couple, send_list, send_count],
        [pltpu.VMEM((1024, 256), jnp.bfloat16)],
        limit=32,
        specs=[VMEM] * 6 + [SMEM],
    )
    came = [
        ring(buffers[0], "east", 1),
        ring(buffers[1], "east", -1),
        ring(buffers[2], "north", 1),
        ring(buffers[3], "north", -1),
    ]
    (heads_out,) = call(back_kernel, [(flat, F32)], [heads])
    (arrivals,) = call(arrive_kernel, [((4, 32, 512), F32)], came)
    return (heads_out.reshape(LZ, CX, CY), moved, arrivals)


def solution(mesh):
    return jax.shard_map(
        on_device,
        mesh=mesh,
        in_specs=(
            P(None, "east", "north"),
            P(None, "east", "north"),
            P(),
            P(None, ("east", "north")),
            P(("east", "north")),
            P(),
            P(None, ("east", "north")),
            P(None, ("east", "north")),
        ),
        out_specs=(
            P(None, "east", "north"),
            P(None, ("east", "north")),
            P(None, None, ("east", "north")),
        ),
        check_vma=False,
    )
```
